256 devices in a mesh: space: 16 (over z_hi, x), chan: 16 (over y, z_lo, core).
Axes of the slice: x: 4, y: 4, z: 8 (z_hi: 4, z_lo: 2; z = z_hi * 2 + z_lo), core: 2. Of those that a mesh axis runs over, the one named last changes fastest.
Arguments:
- features: bfloat16 [49, 128, 2048], P(None, 'chan', 'space'), may hold values from -6 to 6
- ghost_index: int32 [2, 1024], P(None, 'space'), may hold values from 0 to 127
- edge_src: int32 [4096], P('space'), may hold values from 0 to 255
- edge_dst: int32 [4096], P('space'), may hold values from 0 to 127
- edge_count: int32 [16], P('space'), may hold values from 64 to 256, as said below
- rotation: bfloat16 [235, 4096], P(None, 'space'), may hold values from -3 to 3
- distance: float32 [4096], P('space'), may hold values from 1 to 11
- edge_angle: float32 [2, 4096], P(None, 'space'), may hold values from -3.140625 to 3.140625
- radial_weight: bfloat16 [512, 128], replicated, may hold values from -1 to 1
- conv_zero: bfloat16 [7, 128, 896], P(None, 'chan'), may hold values from -0.1875 to 0.1875
- conv_one: bfloat16 [2, 6, 128, 768], P(None, None, 'chan'), may hold values from -0.15625 to 0.15625
- conv_two: bfloat16 [2, 5, 128, 640], P(None, None, 'chan'), may hold values from -0.15625 to 0.15625
- energy_weight: float32 [7, 128], P(None, 'chan'), may hold values from -0.1875 to 0.1875
Outputs:
- atom_energy: float32 [2048], P('space')
- forces: float32 [3, 2048], P(None, 'space')
The draws below stay inside these ranges and needn't reach their ends.
Inputs may be any that keep to these rules, and one draw needn't show every extreme that they name: `edge_count`: at least one slab has all 256 slots live.
All inputs are finite; a program needn't handle non-finite values.
Results may differ from the reference program's by a relative error of at most 0.014.
Values may be sent and summed in bfloat16 or wider, within the bound.
A program may use at most 64 MiB of HBM per device.

```python
import jax
import jax.numpy as jnp

C = 128
RBF = 512
ATOM_DEV = 128
EDGE_DEV = 256
GHOST = 64
ATOMS = 2048
EDGES = 4096
N_SPACE = 16


def draw_edge_count(key, part):
    key = jax.random.fold_in(key, 11)
    slabs = EDGES // EDGE_DEV
    first_key, second_key = jax.random.split(key)
    counts = jax.random.randint(first_key, (slabs,), EDGE_DEV // 4, EDGE_DEV + 1)
    chosen = jax.random.randint(second_key, (), 0, slabs)
    return jnp.where(jnp.arange(slabs) == chosen, EDGE_DEV, counts).astype(jnp.int32)


def place_ends(drawn, key, low, high):
    longest = drawn.shape.index(max(drawn.shape))
    spots = []
    for shift in (0, 1):
        where = [jax.random.randint(jax.random.fold_in(key, axis), (), 0, length) for axis, length in enumerate(drawn.shape)]
        where[longest] = (where[longest] + shift) % drawn.shape[longest]
        spots.append(tuple(where))
    return drawn.at[spots[0]].set(low).at[spots[1]].set(high)


def level_of(rng, shape, shards, least, top_value):
    def one(position, shards_of):
        heights = jax.random.uniform(jax.random.fold_in(jax.random.fold_in(rng, 6), position), (shards_of,), jnp.float32, least / len(shards), top_value / len(shards))
        return jnp.repeat(jnp.exp(heights), shape[position] // shards_of).reshape((-1,) + (1,) * (len(shape) - position - 1))

    gain = one(*shards[0])
    for cut in shards[1:]:
        gain = gain * one(*cut)
    return gain


def gaussian(rng, extent, scale, limit, cuts=(), held_as=jnp.bfloat16):
    level = level_of(rng, extent, cuts, -0.22, 0.18) if cuts else 1.0
    values = jax.random.normal(rng, extent, jnp.float32) * scale * level
    return jnp.minimum(jnp.maximum(values, -limit), limit).astype(held_as)


def setup_inputs(seed: int = 0) -> dict:
    splits = jax.random.split(jax.random.key(seed), 14)
    features = gaussian(splits[0], (49, C, ATOMS), 1.0, 6.0, ((1, 16), (2, 16)))
    ghost_index = place_ends(jax.random.randint(splits[1], (2, GHOST * N_SPACE), 0, ATOM_DEV), jax.random.fold_in(splits[1], 1), 0, ATOM_DEV - 1).astype(jnp.int32)
    edge_src = place_ends(jax.random.randint(splits[2], (EDGES,), 0, 2 * ATOM_DEV), jax.random.fold_in(splits[2], 1), 0, (2 * ATOM_DEV) - 1).astype(jnp.int32)
    edge_dst = place_ends(jax.random.randint(splits[3], (EDGES,), 0, ATOM_DEV), jax.random.fold_in(splits[3], 1), 0, ATOM_DEV - 1).astype(jnp.int32)
    edge_count = draw_edge_count(jax.random.fold_in(splits[13], 71), 0)
    rotation = gaussian(splits[5], (235, EDGES), 0.4, 3.0, ((1, 16),))
    distance = jnp.clip(1.0 + 10.0 * jax.random.uniform(splits[6], (EDGES,), jnp.float32) ** level_of(splits[6], (EDGES,), ((0, 16),), -0.2, 0.2), 1.0, 11.0)
    edge_angle = jnp.clip(jax.random.uniform(splits[7], (2, EDGES), jnp.float32, -3.140625, 3.140625), -3.140625, 3.140625)
    radial_weight = gaussian(splits[8], (RBF, C), 0.16, 1.0)
    conv_zero = gaussian(splits[9], (7, C, 7 * C), (7 * C) ** -0.5, 0.1875, ((1, 16),))
    conv_one = gaussian(splits[10], (2, 6, C, 6 * C), (12 * C) ** -0.5, 0.15625, ((2, 16),))
    conv_two = gaussian(splits[11], (2, 5, C, 5 * C), (10 * C) ** -0.5, 0.15625, ((2, 16),))
    energy_weight = gaussian(splits[12], (7, C), (7 * C) ** -0.5, 0.1875, ((1, 16),), jnp.float32)
    return dict(features=features, ghost_index=ghost_index, edge_src=edge_src, edge_dst=edge_dst, edge_count=edge_count, rotation=rotation, distance=distance, edge_angle=edge_angle, radial_weight=radial_weight, conv_zero=conv_zero, conv_one=conv_one, conv_two=conv_two, energy_weight=energy_weight)


CUTOFF = 12.0
SHARPNESS = 2.0


def degree_height(degree):
    return min(2 * degree + 1, 5)


def block_offsets():
    offsets = []
    cursor = 0
    for degree in range(7):
        offsets.append(cursor)
        cursor = cursor + degree_height(degree) * (2 * degree + 1)
    return offsets


def group_index(degree, order_slot):
    if order_slot == 0:
        return degree
    if order_slot == 1:
        return 7 + degree - 1
    if order_slot == 2:
        return 13 + degree - 1
    if order_slot == 3:
        return 19 + degree - 2
    return 24 + degree - 2


def rotation_block(rotation, degree):
    offsets = block_offsets()
    height = degree_height(degree)
    across = 2 * degree + 1
    return rotation[offsets[degree]:offsets[degree] + height * across].reshape(height, across, -1).astype(jnp.float32)


def rotate_edges(rotation, source):
    pieces = [None] * 29
    for degree in range(7):
        block = rotation_block(rotation, degree)
        coeffs = source[degree * degree:(degree + 1) * (degree + 1)].astype(jnp.float32)
        turned = jnp.einsum('rke,kce->rce', block, coeffs)
        for order_slot in range(degree_height(degree)):
            pieces[group_index(degree, order_slot)] = turned[order_slot]
    return jnp.stack(pieces)


def turn_back(rotation, grouped):
    result = []
    for degree in range(7):
        block = rotation_block(rotation, degree)
        stacked = jnp.stack([grouped[group_index(degree, order_slot)] for order_slot in range(degree_height(degree))])
        result.append(jnp.einsum('rke,rce->kce', block, stacked))
    return result


def apply_weight(weight, inputs):
    span = inputs.shape[-1]
    out_rows = weight.shape[-3] * weight.shape[-2]
    product = jnp.dot(weight.reshape(out_rows, -1), inputs.reshape(-1, span), preferred_element_type=jnp.float32)
    return product.reshape(weight.shape[-3], weight.shape[-2], span)


def convolve(conv_zero, conv_one, conv_two, gated):
    zero_out = apply_weight(conv_zero, gated[0:7])
    plus_one = apply_weight(conv_one[0], gated[7:13]) - apply_weight(conv_one[1], gated[13:19])
    minus_one = apply_weight(conv_one[0], gated[13:19]) + apply_weight(conv_one[1], gated[7:13])
    plus_two = apply_weight(conv_two[0], gated[19:24]) - apply_weight(conv_two[1], gated[24:29])
    minus_two = apply_weight(conv_two[0], gated[24:29]) + apply_weight(conv_two[1], gated[19:24])
    return jnp.concatenate([zero_out, plus_one, minus_one, plus_two, minus_two], axis=0)


def apply_transposed(weight, grads):
    span = grads.shape[-1]
    out_rows = weight.shape[-3] * weight.shape[-2]
    flat = weight.reshape(out_rows, -1)
    product = jnp.dot(flat.T, grads.reshape(out_rows, span), preferred_element_type=jnp.float32)
    return product.reshape(weight.shape[-3], -1, span)


def convolve_adjoint(conv_zero, conv_one, conv_two, grads):
    zero_in = apply_transposed(conv_zero, grads[0:7])
    plus_one = apply_transposed(conv_one[0], grads[7:13]) + apply_transposed(conv_one[1], grads[13:19])
    minus_one = apply_transposed(conv_one[0], grads[13:19]) - apply_transposed(conv_one[1], grads[7:13])
    plus_two = apply_transposed(conv_two[0], grads[19:24]) + apply_transposed(conv_two[1], grads[24:29])
    minus_two = apply_transposed(conv_two[0], grads[24:29]) - apply_transposed(conv_two[1], grads[19:24])
    return jnp.concatenate([zero_in, plus_one, minus_one, plus_two, minus_two], axis=0)


def silu_slope(values):
    sigma = jax.nn.sigmoid(values)
    return sigma * (1.0 + values * (1.0 - sigma))


def readout(hidden, energy_weight):
    leading = hidden[0][0]
    energy = jnp.sum(energy_weight[0][:, None] * jax.nn.silu(leading), axis=0)
    grads = [(energy_weight[0][:, None] * silu_slope(leading))[None]]
    for degree in range(1, 7):
        block = hidden[degree]
        square = jnp.sum(block * block, axis=0)
        energy = energy + jnp.sum(energy_weight[degree][:, None] * jnp.log(1.0 + square), axis=0)
        grads.append(energy_weight[degree][None, :, None] * 2.0 * block / (1.0 + square)[None])
    return energy, grads


def radial_basis(distance, count):
    centers = CUTOFF * jnp.arange(count, dtype=jnp.float32) / (count - 1)
    offset_grid = distance[None, :] - centers[:, None]
    basis = jnp.exp(-SHARPNESS * offset_grid * offset_grid)
    slope = -2.0 * SHARPNESS * offset_grid * basis
    return basis, slope


def reference(features, ghost_index, edge_src, edge_dst, edge_count, rotation, distance, edge_angle, radial_weight, conv_zero, conv_one, conv_two, energy_weight):
    edge_dev = jnp.arange(EDGES, dtype=jnp.int32) // EDGE_DEV
    left_dev = (edge_dev + N_SPACE - 1) % N_SPACE
    right_dev = (edge_dev + 1) % N_SPACE
    near_slot = jnp.clip(edge_src - ATOM_DEV, 0, GHOST - 1).astype(jnp.int32)
    far_slot = jnp.clip(edge_src - ATOM_DEV - GHOST, 0, GHOST - 1).astype(jnp.int32)
    lent_left = left_dev * ATOM_DEV + ghost_index[0][left_dev * GHOST + near_slot]
    lent_right = right_dev * ATOM_DEV + ghost_index[1][right_dev * GHOST + far_slot]
    source = jnp.where(edge_src < ATOM_DEV, edge_dev * ATOM_DEV + edge_src, jnp.where(edge_src < ATOM_DEV + GHOST, lent_left, lent_right)).astype(jnp.int32)
    target = (edge_dev * ATOM_DEV + edge_dst).astype(jnp.int32)
    live = ((jnp.arange(EDGES, dtype=jnp.int32) % EDGE_DEV) < edge_count[edge_dev]).astype(jnp.float32)

    turned = rotate_edges(rotation, features[:, :, source]).astype(jnp.bfloat16)
    basis, slope = radial_basis(distance, RBF)
    preact = jnp.dot(radial_weight.T, basis.astype(jnp.bfloat16), preferred_element_type=jnp.float32)
    gate = jax.nn.silu(preact) * live[None]
    gated = (turned.astype(jnp.float32) * gate[None]).astype(jnp.bfloat16)
    outputs = convolve(conv_zero, conv_one, conv_two, gated)
    pieces = turn_back(rotation, outputs)
    hidden = []
    for degree in range(7):
        summed = jnp.zeros((2 * degree + 1, C, ATOMS), jnp.float32).at[:, :, target].add(pieces[degree])
        hidden.append(features[degree * degree:(degree + 1) * (degree + 1)].astype(jnp.float32) + summed)
    atom_energy, grads = readout(hidden, energy_weight)
    grads_edge = jnp.concatenate([grad_block[:, :, target] for grad_block in grads], axis=0)
    out_grads = rotate_edges(rotation, grads_edge).astype(jnp.bfloat16)
    dgated = convolve_adjoint(conv_zero, conv_one, conv_two, out_grads)
    pull_weight = jnp.dot(radial_weight.T, slope.astype(jnp.bfloat16), preferred_element_type=jnp.float32)
    steep = silu_slope(preact) * live[None] * pull_weight
    gate_grad = jnp.sum(turned.astype(jnp.float32) * dgated, axis=0)
    pull = jnp.sum(gate_grad * steep, axis=0)
    polar = edge_angle[0]
    azimuth = edge_angle[1]
    unit = jnp.stack([jnp.sin(polar) * jnp.cos(azimuth), jnp.sin(polar) * jnp.sin(azimuth), jnp.cos(polar)])
    push = pull[None] * unit
    forces = jnp.zeros((3, ATOMS), jnp.float32).at[:, target].add(-push).at[:, source].add(push)
    return atom_energy, forces
```

```python
import jax
import jax.numpy as jnp
from jax import lax
from jax.experimental import pallas as pl
from jax.experimental.pallas import tpu as pltpu
from jax.sharding import PartitionSpec as P

MESH = pl.DeviceIdType.MESH
F32 = jnp.float32
BF16 = jnp.bfloat16
NC = 16
CHUNKS = ((0, 64), (64, 96), (160, 80))
HEIGHT = [min(2 * l + 1, 5) for l in range(7)]
OFFSET = [sum(HEIGHT[m] * (2 * m + 1) for m in range(l)) for l in range(7)]
FIRST = (0, 7, 13, 19, 24)
LEAST = (0, 1, 1, 2, 2)


def row_of(degree, order):
    return FIRST[order] + degree - LEAST[order]


def padded_row(row):
    return row if row < 7 else row + 1


def dot(a, b):
    return jnp.dot(a, b, preferred_element_type=F32)


def dot_nt(a, b):
    return lax.dot_general(a, b, (((1,), (1,)), ((), ())), preferred_element_type=F32)


def split(x):
    hi = x.astype(BF16)
    return hi, (x - hi.astype(F32)).astype(BF16)


def kernel(
    feat, gidx, esrc, edst, count, rot, dist, ang, radial, wzero, wone, wtwo, eweight,
    energy_out, force_out,
    mine, mine_g, ghost, ghost_g, wz, w1, w2, rf, r3, s3, t3, snd, every, gate, x, ob, orecv,
    pf, pt, fcoef, nconst, ewcol, red, fsend, frecv,
    g_send, g_recv, w_send, w_recv, a_send, a_recv, o_send, o_recv, r_send, r_recv, f_send, f_recv,
):
    space = lax.axis_index("space")
    chan = lax.axis_index("chan")
    n_space = lax.axis_size("space")
    after = lax.rem(space + 1, n_space)
    before = lax.rem(space + n_space - 1, n_space)
    core = lax.rem(chan, 2)
    other = 1 - core
    sibling = chan + 1 - 2 * core

    def remote(src, dst, send, recv, where):
        return pltpu.make_async_remote_copy(
            src_ref=src, dst_ref=dst, send_sem=send, recv_sem=recv, device_id=where, device_id_type=MESH
        )

    barrier = pltpu.get_barrier_semaphore()

    def greet(d, carry):
        pl.semaphore_signal(barrier, inc=1, device_id=(space, lax.rem(chan + d, NC)), device_id_type=MESH)
        return carry

    lax.fori_loop(1, NC, greet, 0)
    pl.semaphore_signal(barrier, inc=1, device_id=(after, chan), device_id_type=MESH)
    pl.semaphore_signal(barrier, inc=1, device_id=(before, chan), device_id_type=MESH)

    own = feat[...].astype(F32).reshape(392, 128)
    fcoef[...] = own
    mine[0:392, :] = own.astype(BF16)
    mine[384:400, :] = jnp.concatenate([own[384:392], jnp.zeros((8, 128), F32)], axis=0).astype(BF16)
    mine_g[...] = jnp.zeros((8, 128), jnp.int32)
    mine_g[0:2, 0:64] = gidx[...]
    pl.semaphore_wait(barrier, NC + 1)

    exchange = [
        remote(mine, ghost.at[0], g_send.at[0], g_recv.at[0], (after, chan)),
        remote(mine, ghost.at[1], g_send.at[1], g_recv.at[1], (before, chan)),
        remote(mine_g, ghost_g.at[0], g_send.at[2], g_recv.at[2], (after, chan)),
        remote(mine_g, ghost_g.at[1], g_send.at[3], g_recv.at[3], (before, chan)),
    ]
    for copy in exchange:
        copy.start()

    wz[core] = jnp.concatenate(
        [wzero[...].astype(F32).reshape(56, 896), jnp.zeros((8, 896), F32)], axis=0
    ).astype(BF16)
    w1[core] = wone[...].astype(F32).reshape(96, 768).astype(BF16)
    w2[core] = wtwo[...].astype(F32).reshape(80, 640).astype(BF16)
    weights = [
        remote(w.at[core], w.at[core], w_send.at[i], w_recv.at[i], (space, sibling))
        for i, w in enumerate((wz, w1, w2))
    ]
    for copy in weights:
        copy.start()

    rf[0:235, :] = rot[...].astype(F32)

    def spread(i, carry):
        for j in range(5):
            row = i * 5 + j
            line = rf[pl.ds(row, 1), :]
            r3[0, row] = jnp.broadcast_to(line[:, :128], (8, 128))
            r3[1, row] = jnp.broadcast_to(line[:, 128:], (8, 128))
        return carry

    lax.fori_loop(0, 47, spread, 0)

    atom_row = lax.broadcasted_iota(jnp.int32, (128, 256), 0)
    source = esrc[...]
    target_hot = (edst[...] == atom_row).astype(F32)
    source_hot = (source == atom_row).astype(F32)
    nconst[0] = source_hot.astype(BF16)
    nconst[3] = target_hot.astype(BF16)
    base_coeffs = dot(mine[...], nconst[0])

    live = (lax.broadcasted_iota(jnp.int32, (1, 128), 1) + core * 128 < count[...]).astype(F32)
    center = 12.0 * lax.broadcasted_iota(jnp.int32, (512, 128), 0).astype(F32) / 511.0
    grid = dist[pl.ds(core, 1), :] - center
    basis = jnp.exp(-2.0 * grid * grid)
    slope = -4.0 * grid * basis
    both = jnp.concatenate([basis.astype(BF16), slope.astype(BF16)], axis=1)
    radial_out = lax.dot_general(
        radial[...], both, (((0,), (0,)), ((), ())), preferred_element_type=F32
    )
    preact = radial_out[:, :128]
    sigma = jax.nn.sigmoid(preact)
    gate[0] = preact * sigma * live
    gate[1] = sigma * (1.0 + preact * (1.0 - sigma)) * live * radial_out[:, 128:]

    eye = (
        lax.broadcasted_iota(jnp.int32, (8, 8), 0) == lax.broadcasted_iota(jnp.int32, (8, 8), 1)
    ).astype(F32)
    for degree in range(7):
        column = jnp.sum(eweight[degree : degree + 1, :] * eye, axis=1, keepdims=True)
        ewcol[degree] = jnp.broadcast_to(column, (8, 128))

    polar, azimuth = ang[0:1, :], ang[1:2, :]
    unit = [jnp.sin(polar) * jnp.cos(azimuth), jnp.sin(polar) * jnp.sin(azimuth), jnp.cos(polar)]

    slot_row = lax.broadcasted_iota(jnp.int32, (64, 256), 0)
    atom_lane = lax.broadcasted_iota(jnp.int32, (128, 64), 0)
    for copy in exchange:
        copy.wait_recv()
    coeffs = base_coeffs
    for side in range(2):
        slot_hot = (source - (128 + 64 * side) == slot_row).astype(F32).astype(BF16)
        lent_hot = (ghost_g[side, side : side + 1, 0:64] == atom_lane).astype(F32).astype(BF16)
        nconst[1 + side] = dot(lent_hot, slot_hot).astype(BF16)
        coeffs = coeffs + dot(ghost[side], nconst[1 + side])
    s3[0] = coeffs[0:392, :128].reshape(49, 8, 128)
    s3[1] = coeffs[0:392, 128:].reshape(49, 8, 128)

    def transfers(d, g):
        first, rows = CHUNKS[g]
        to = lax.rem(chan + d, NC)
        return remote(
            snd.at[lax.rem(to, 2), pl.ds(first, rows)],
            every.at[chan, pl.ds(first, rows)],
            a_send.at[d - 1, g],
            a_recv.at[d - 1, g],
            (space, to),
        )

    t3[:, 7] = jnp.zeros((2, 8, 128), F32)
    for g in range(3):
        for order in ((0,), (1, 2), (3, 4))[g]:
            for degree in range(LEAST[order], 7):
                width = 2 * degree + 1
                at = OFFSET[degree] + order * width
                row = padded_row(row_of(degree, order))
                for half in range(2):
                    t3[half, row] = jnp.sum(
                        r3[half, at : at + width] * s3[half, degree * degree : (degree + 1) ** 2], axis=0
                    )
        first, rows = CHUNKS[g]
        for half in range(2):
            snd[half, first : first + rows] = (
                t3[half, first // 8 : (first + rows) // 8].reshape(rows, 128).astype(BF16)
            )
        every[chan, first : first + rows] = snd[core, first : first + rows]

        def launch(d, carry):
            transfers(d, g).start()
            return carry

        lax.fori_loop(1, NC, launch, 0)

    for copy in weights:
        copy.wait_recv()
    for g in range(3):

        def arrive(d, carry):
            transfers(d, g).wait_recv()
            return carry

        lax.fori_loop(1, NC, arrive, 0)
        first, rows = CHUNKS[g]
        for t in range(first, first + rows, 16):
            pair = every[:, t : t + 16, :].astype(F32).reshape(NC, 2, 8, 128)
            for i in range(2):
                row = t // 8 + i
                if row == 7:
                    continue
                turned = pair[:, i].reshape(128, 128)
                x[row, :, 0:128] = (turned * gate[0]).astype(BF16)
                x[row, :, 128:256] = (turned * gate[1]).astype(BF16)
        if g == 0:
            y = dot(wz[...].reshape(128, 896), x[0:7].reshape(896, 256))
            for c in range(2):
                ob[c, 0:7] = y[64 * c : 64 * c + 56].reshape(7, 8, 256)
        else:
            w, n, lo = ((w1, 6, 8), (w2, 5, 20))[g - 1]
            flat = w[...].reshape(32 * n, 128 * n)
            plus = dot(flat, x[lo : lo + n].reshape(128 * n, 256))
            minus = dot(flat, x[lo + n : lo + 2 * n].reshape(128 * n, 256))
            for c in range(2):
                real, imag = 16 * n * c, 16 * n * c + 8 * n
                ob[c, lo - 1 : lo - 1 + n] = (
                    plus[real : real + 8 * n] - minus[imag : imag + 8 * n]
                ).reshape(n, 8, 256)
                ob[c, lo - 1 + n : lo - 1 + 2 * n] = (
                    minus[real : real + 8 * n] + plus[imag : imag + 8 * n]
                ).reshape(n, 8, 256)
    swap = remote(ob.at[other], orecv, o_send, o_recv, (space, sibling))
    swap.start()

    def turn_back(half, rows):
        for degree in range(7):
            width = 2 * degree + 1
            ahead = back = None
            for order in range(HEIGHT[degree]):
                at = OFFSET[degree] + order * width
                block = r3[half, at : at + width]
                line = rows(row_of(degree, order))
                one, two = block * line[:, :128], block * line[:, 128:]
                ahead = one if ahead is None else ahead + one
                back = two if back is None else back + two
            pf[half, degree * degree : (degree + 1) ** 2] = ahead
            pt[half, degree * degree : (degree + 1) ** 2] = back

    turn_back(core, lambda row: ob[core, row])
    swap.wait_recv()
    turn_back(other, lambda row: orecv[row])

    total = fcoef[...]
    for half in range(2):
        hi, lo = split(pf[half].reshape(392, 128))
        hot = nconst[3, :, 128 * half : 128 * half + 128]
        total = total + dot_nt(
            jnp.concatenate([hi, lo], axis=1), jnp.concatenate([hot, hot], axis=1)
        )
    hidden = total.reshape(49, 8, 128)
    lead = hidden[0]
    sigma = jax.nn.sigmoid(lead)
    energy = ewcol[0] * (lead * sigma)
    grads = [(ewcol[0] * (sigma * (1.0 + lead * (1.0 - sigma))))[None]]
    for degree in range(1, 7):
        block = hidden[degree * degree : (degree + 1) ** 2]
        square = 1.0 + jnp.sum(block * block, axis=0)
        energy = energy + ewcol[degree] * jnp.log(square)
        grads.append((ewcol[degree] * 2.0 / square) * block)
    hi, lo = split(jnp.concatenate(grads, axis=0).reshape(392, 128))
    hot = nconst[3]
    edge_grads = dot(
        jnp.concatenate([hi, lo], axis=1), jnp.concatenate([hot, hot], axis=0)
    )
    parts = []
    for half in range(2):
        block = edge_grads[:, 128 * half : 128 * half + 128].reshape(49, 8, 128)
        parts.append(jnp.sum(jnp.sum(block * pt[half], axis=0), axis=0, keepdims=True))
    parts.append(jnp.sum(energy, axis=0, keepdims=True))
    red[chan] = jnp.concatenate(parts + [jnp.zeros((5, 128), F32)], axis=0)

    def sums(d):
        to = lax.rem(chan + d, NC)
        return remote(red.at[chan], red.at[chan], r_send.at[d - 1], r_recv.at[d - 1], (space, to))

    def launch_sums(d, carry):
        sums(d).start()
        return carry

    def arrive_sums(d, carry):
        sums(d).wait_recv()
        return carry

    lax.fori_loop(1, NC, launch_sums, 0)
    lax.fori_loop(1, NC, arrive_sums, 0)
    summed = jnp.sum(red[...], axis=0)
    energy_out[...] = summed[2:3]
    pull = jnp.concatenate([summed[0:1], summed[1:2]], axis=1)
    push = jnp.concatenate([pull * u for u in unit] + [jnp.zeros((5, 256), F32)], axis=0)
    hi, lo = split(push)
    hilo = jnp.concatenate([hi.astype(F32), lo.astype(F32)], axis=0).astype(BF16)
    owed = []
    for side in range(2):
        part = dot_nt(hilo, nconst[1 + side])
        fsend[side] = part[0:8] + part[8:16]
    back = [
        remote(fsend.at[0], frecv.at[0], f_send.at[0], f_recv.at[0], (before, chan)),
        remote(fsend.at[1], frecv.at[1], f_send.at[1], f_recv.at[1], (after, chan)),
    ]
    for copy in back:
        copy.start()
    part = dot_nt(hilo, nconst[0]) - dot_nt(hilo, nconst[3])
    part = part[0:8] + part[8:16]
    for copy in back:
        copy.wait_recv()
    force_out[...] = (part + frecv[0] + frecv[1])[0:3]

    for copy in exchange + weights + [swap] + back:
        copy.wait_send()

    def drain(d, carry):
        for g in range(3):
            transfers(d, g).wait_send()
        sums(d).wait_send()
        return carry

    lax.fori_loop(1, NC, drain, 0)


def local(
    features, ghost_index, edge_src, edge_dst, edge_count, rotation, distance, edge_angle,
    radial_weight, conv_zero, conv_one, conv_two, energy_weight,
):
    vmem = pl.BlockSpec(memory_space=pltpu.VMEM)
    dma = pltpu.SemaphoreType.DMA
    energy, forces = pl.pallas_call(
        kernel,
        out_shape=(jax.ShapeDtypeStruct((1, 128), F32), jax.ShapeDtypeStruct((3, 128), F32)),
        in_specs=[vmem] * 13,
        out_specs=(vmem, vmem),
        scratch_shapes=[
            pltpu.VMEM((400, 128), BF16),
            pltpu.VMEM((8, 128), jnp.int32),
            pltpu.VMEM((2, 400, 128), BF16),
            pltpu.VMEM((2, 8, 128), jnp.int32),
            pltpu.VMEM((2, 64, 896), BF16),
            pltpu.VMEM((2, 96, 768), BF16),
            pltpu.VMEM((2, 80, 640), BF16),
            pltpu.VMEM((240, 256), F32),
            pltpu.VMEM((2, 235, 8, 128), F32),
            pltpu.VMEM((2, 49, 8, 128), F32),
            pltpu.VMEM((2, 30, 8, 128), F32),
            pltpu.VMEM((2, 240, 128), BF16),
            pltpu.VMEM((NC, 240, 128), BF16),
            pltpu.VMEM((2, 128, 128), F32),
            pltpu.VMEM((30, 128, 256), BF16),
            pltpu.VMEM((2, 29, 8, 256), F32),
            pltpu.VMEM((29, 8, 256), F32),
            pltpu.VMEM((2, 49, 8, 128), F32),
            pltpu.VMEM((2, 49, 8, 128), F32),
            pltpu.VMEM((392, 128), F32),
            pltpu.VMEM((4, 128, 256), BF16),
            pltpu.VMEM((7, 8, 128), F32),
            pltpu.VMEM((NC, 8, 128), F32),
            pltpu.VMEM((2, 8, 128), F32),
            pltpu.VMEM((2, 8, 128), F32),
            dma((4,)),
            dma((4,)),
            dma((3,)),
            dma((3,)),
            dma((NC - 1, 3)),
            dma((NC - 1, 3)),
            dma,
            dma,
            dma((NC - 1,)),
            dma((NC - 1,)),
            dma((2,)),
            dma((2,)),
        ],
        compiler_params=pltpu.CompilerParams(
            collective_id=0, has_side_effects=True, vmem_limit_bytes=48 * 1024 * 1024
        ),
        cost_estimate=pl.CostEstimate(flops=400_000_000, bytes_accessed=3_000_000, transcendentals=200_000),
    )(
        features,
        ghost_index,
        edge_src.reshape(1, 256),
        edge_dst.reshape(1, 256),
        edge_count.reshape(1, 1),
        rotation,
        distance.reshape(2, 128),
        edge_angle,
        radial_weight,
        conv_zero,
        conv_one,
        conv_two,
        energy_weight,
    )
    return (energy.reshape(128), forces)


def solution(mesh):
    in_specs = (
        P(None, "chan", "space"),
        P(None, "space"),
        P("space"),
        P("space"),
        P("space"),
        P(None, "space"),
        P("space"),
        P(None, "space"),
        P(),
        P(None, "chan", None),
        P(None, None, "chan", None),
        P(None, None, "chan", None),
        P(None, "chan"),
    )
    out_specs = (P("space"), P(None, "space"))
    return jax.shard_map(local, mesh=mesh, in_specs=in_specs, out_specs=out_specs, check_vma=False)
```

```python
import jax
import jax.numpy as jnp
from jax import lax
from jax.experimental import pallas as pl
from jax.experimental.pallas import tpu as pltpu
from jax.sharding import PartitionSpec as P

MESH = pl.DeviceIdType.MESH
F32 = jnp.float32
BF16 = jnp.bfloat16
NC = 16
CHUNKS = ((0, 64), (64, 96), (160, 80))
HEIGHT = [min(2 * l + 1, 5) for l in range(7)]
OFFSET = [sum(HEIGHT[m] * (2 * m + 1) for m in range(l)) for l in range(7)]
FIRST = (0, 7, 13, 19, 24)
LEAST = (0, 1, 1, 2, 2)
FETCH_ORDER = (0, 1, 9, 10, 11, 5, 2, 3, 4, 6, 8, 12, 7)


def row_of(degree, order):
    return FIRST[order] + degree - LEAST[order]


def padded_row(row):
    return row if row < 7 else row + 1


def dot(a, b):
    return jnp.dot(a, b, preferred_element_type=F32)


def dot_nt(a, b):
    return lax.dot_general(a, b, (((1,), (1,)), ((), ())), preferred_element_type=F32)


def split(x):
    hi = x.astype(BF16)
    return hi, (x - hi.astype(F32)).astype(BF16)


def kernel(*refs):
    held = refs[:13]
    energy_out, force_out = refs[13:15]
    feat, gidx, esrc, edst, count, rot, dist, ang, radial, wzero, wone, wtwo, eweight = refs[15:28]
    (
        coef, base, shot, mine, mine_g, ghost, ghost_g, wz, w1, w2, rf, r3, s3, t3, snd, every, gate, x, ob, orecv,
        pf, pt, fcoef, nconst, ewcol, red, fsend, frecv,
        g_send, g_recv, w_send, w_recv, a_send, a_recv, o_send, o_recv, r_send, r_recv, f_send, f_recv, h_recv,
    ) = refs[28:]
    fetch = [
        pltpu.make_async_copy(src, dst, h_recv.at[i])
        for i, (src, dst) in enumerate(zip(held, refs[15:28]))
    ]
    for i in FETCH_ORDER:
        fetch[i].start()
    space = lax.axis_index("space")
    chan = lax.axis_index("chan")
    n_space = lax.axis_size("space")
    after = lax.rem(space + 1, n_space)
    before = lax.rem(space + n_space - 1, n_space)
    core = lax.rem(chan, 2)
    other = 1 - core
    sibling = chan + 1 - 2 * core

    def remote(src, dst, send, recv, where):
        return pltpu.make_async_remote_copy(
            src_ref=src, dst_ref=dst, send_sem=send, recv_sem=recv, device_id=where, device_id_type=MESH
        )

    barrier = pltpu.get_barrier_semaphore()

    def greet(d, carry):
        pl.semaphore_signal(barrier, inc=1, device_id=(space, lax.rem(chan + d, NC)), device_id_type=MESH)
        return carry

    lax.fori_loop(1, NC, greet, 0)
    pl.semaphore_signal(barrier, inc=1, device_id=(after, chan), device_id_type=MESH)
    pl.semaphore_signal(barrier, inc=1, device_id=(before, chan), device_id_type=MESH)

    fetch[0].wait()
    fetch[1].wait()
    own = feat[...].astype(F32).reshape(392, 128)
    fcoef[...] = own
    own = jnp.concatenate([own, jnp.zeros((24, 128), F32)], axis=0).astype(BF16)
    coef[...] = own
    lend_row = lax.broadcasted_iota(jnp.int32, (256, 256), 0)
    lend_at = jnp.concatenate(
        [gidx[0:1, :], gidx[0:1, :] + 128, gidx[1:2, :], gidx[1:2, :] + 128], axis=1
    )
    lend_hot = (lend_at == lend_row).astype(F32).astype(BF16)
    lent = dot(jnp.concatenate([own[:208], own[208:]], axis=1), lend_hot).astype(BF16)
    mine[0] = lent[:, :128]
    mine[1] = lent[:, 128:]
    mine_g[...] = jnp.zeros((8, 128), jnp.int32)
    mine_g[0:2, 0:64] = gidx[...]
    pl.semaphore_wait(barrier, NC + 1)

    exchange = [
        remote(mine.at[0], ghost.at[0], g_send.at[0], g_recv.at[0], (after, chan)),
        remote(mine.at[1], ghost.at[1], g_send.at[1], g_recv.at[1], (before, chan)),
        remote(mine_g, ghost_g.at[0], g_send.at[2], g_recv.at[2], (after, chan)),
        remote(mine_g, ghost_g.at[1], g_send.at[3], g_recv.at[3], (before, chan)),
    ]
    for copy in exchange:
        copy.start()

    for i in (9, 10, 11):
        fetch[i].wait()
    wz[core] = jnp.concatenate(
        [wzero[...].astype(F32).reshape(56, 896), jnp.zeros((8, 896), F32)], axis=0
    ).astype(BF16)
    w1[core] = wone[...].astype(F32).reshape(96, 768).astype(BF16)
    w2[core] = wtwo[...].astype(F32).reshape(80, 640).astype(BF16)
    weights = [
        remote(w.at[core], w.at[core], w_send.at[i], w_recv.at[i], (space, sibling))
        for i, w in enumerate((wz, w1, w2))
    ]
    for copy in weights:
        copy.start()

    fetch[5].wait()
    rf[0:235, :] = rot[...].astype(F32)

    def spread(i, carry):
        for j in range(5):
            row = i * 5 + j
            line = rf[pl.ds(row, 1), :]
            r3[0, row] = jnp.broadcast_to(line[:, :128], (8, 128))
            r3[1, row] = jnp.broadcast_to(line[:, 128:], (8, 128))
        return carry

    lax.fori_loop(0, 47, spread, 0)

    for i in (2, 3, 4, 6, 7, 8, 12):
        fetch[i].wait()
    atom_row = lax.broadcasted_iota(jnp.int32, (128, 256), 0)
    source = esrc[...]
    target_hot = (edst[...] == atom_row).astype(F32)
    source_hot = (source == atom_row).astype(F32)
    nconst[0] = source_hot.astype(BF16)
    nconst[3] = target_hot.astype(BF16)
    base[...] = dot(coef[...], nconst[0])
    slot_row = lax.broadcasted_iota(jnp.int32, (256, 256), 0)
    slot_of = slot_row - 64 * (slot_row // 64) + 64 * (slot_row // 128)
    upper = (slot_row // 64) % 2
    for half in range(2):
        shot[:, 256 * half : 256 * half + 256] = (
            (source - 128 == jnp.where(upper == half, slot_of, -1000)).astype(F32).astype(BF16)
        )

    live = (lax.broadcasted_iota(jnp.int32, (1, 128), 1) + core * 128 < count[0]).astype(F32)
    center = 12.0 * lax.broadcasted_iota(jnp.int32, (512, 128), 0).astype(F32) / 511.0
    grid = dist[pl.ds(core, 1), :] - center
    basis = jnp.exp(-2.0 * grid * grid)
    slope = -4.0 * grid * basis
    both = jnp.concatenate([basis.astype(BF16), slope.astype(BF16)], axis=1)
    radial_out = lax.dot_general(
        radial[...], both, (((0,), (0,)), ((), ())), preferred_element_type=F32
    )
    preact = radial_out[:, :128]
    sigma = jax.nn.sigmoid(preact)
    gate[0] = preact * sigma * live
    gate[1] = sigma * (1.0 + preact * (1.0 - sigma)) * live * radial_out[:, 128:]

    eye = (
        lax.broadcasted_iota(jnp.int32, (8, 8), 0) == lax.broadcasted_iota(jnp.int32, (8, 8), 1)
    ).astype(F32)
    for degree in range(7):
        column = jnp.sum(eweight[degree : degree + 1, :] * eye, axis=1, keepdims=True)
        ewcol[degree] = jnp.broadcast_to(column, (8, 128))

    polar, azimuth = ang[0:1, :], ang[1:2, :]
    unit = [jnp.sin(polar) * jnp.cos(azimuth), jnp.sin(polar) * jnp.sin(azimuth), jnp.cos(polar)]

    for copy in exchange[:2]:
        copy.wait_recv()
    lent = dot(jnp.concatenate([ghost[0], ghost[1]], axis=1), shot[...])
    for half in range(2):
        at = 128 * half
        s3[half, 0:26] = (base[0:208, at : at + 128] + lent[:, at : at + 128]).reshape(26, 8, 128)
        s3[half, 26:49] = (
            base[208:392, at : at + 128] + lent[0:184, 256 + at : 384 + at]
        ).reshape(23, 8, 128)

    along, deep = lax.div(chan, 4), lax.rem(lax.div(chan, 2), 2)

    def peer(dy, dz, c):
        return lax.rem(along + dy, 4) * 4 + lax.rem(deep + dz, 2) * 2 + c

    def piece_of(ref, g, first, count):
        start, rows = CHUNKS[g]
        return ref.at[pl.ds(first, count), pl.ds(start, rows)]

    def own_sends(g):
        plans = [(sibling, other, 0)]
        for c in range(2):
            plans.append((peer(0, 1, c), c, 1 + core))
            plans.append((peer(1, 0, c), c, 3 + core))
            plans.append((peer(3, 0, c), c, 5 + core))
        return [
            remote(piece_of(snd, g, half, 1), piece_of(every, g, chan, 1), a_send.at[i, g], a_recv.at[kind, g], (space, to))
            for i, (to, half, kind) in enumerate(plans)
        ]

    def relay(g, slot, kind, first, count, to):
        return remote(
            piece_of(every, g, first, count), piece_of(every, g, first, count), a_send.at[slot, g], a_recv.at[kind, g], (space, to)
        )

    ahead, behind, across = peer(1, 0, core), peer(3, 0, core), peer(0, 1, core)
    paths = [
        (peer(0, 1, 0), 2, ahead),
        (peer(0, 1, 0), 2, behind),
        (peer(3, 0, 0), 1, ahead),
        (peer(1, 0, 1), 1, behind),
        (peer(2, 0, 0), 1, across),
        (peer(2, 0, 1), 1, across),
    ]

    def passed(g, i):
        return relay(g, 7 + i, 7 + i, *paths[i])

    def landed(g, kind, first, count):
        relay(g, 0, kind, first, count, sibling).wait_recv()

    t3[:, 7] = jnp.zeros((2, 8, 128), F32)
    for g in range(3):
        for order in ((0,), (1, 2), (3, 4))[g]:
            for degree in range(LEAST[order], 7):
                width = 2 * degree + 1
                at = OFFSET[degree] + order * width
                row = padded_row(row_of(degree, order))
                for half in range(2):
                    t3[half, row] = jnp.sum(
                        r3[half, at : at + width] * s3[half, degree * degree : (degree + 1) ** 2], axis=0
                    )
        first, rows = CHUNKS[g]
        for half in range(2):
            snd[half, first : first + rows] = (
                t3[half, first // 8 : (first + rows) // 8].reshape(rows, 128).astype(BF16)
            )
        every[chan, first : first + rows] = snd[core, first : first + rows]

        for copy in own_sends(g):
            copy.start()

    for g in range(3):
        for c in range(2):
            landed(g, 1 + c, peer(0, 1, c), 1)
        passed(g, 0).start()
        passed(g, 1).start()
        landed(g, 3, peer(3, 0, 0), 1)
        passed(g, 2).start()
        landed(g, 6, peer(1, 0, 1), 1)
        passed(g, 3).start()
    for g in range(3):
        landed(g, 9, peer(2, 0, 0), 1)
        passed(g, 4).start()
        landed(g, 10, peer(2, 0, 1), 1)
        passed(g, 5).start()

    for copy in exchange[2:]:
        copy.wait_recv()
    slot_row = lax.broadcasted_iota(jnp.int32, (64, 256), 0)
    atom_lane = lax.broadcasted_iota(jnp.int32, (128, 64), 0)
    for side in range(2):
        slot_hot = (source - (128 + 64 * side) == slot_row).astype(F32).astype(BF16)
        lent_hot = (ghost_g[side, side : side + 1, 0:64] == atom_lane).astype(F32).astype(BF16)
        nconst[1 + side] = dot(lent_hot, slot_hot).astype(BF16)
    for copy in weights:
        copy.wait_recv()
    for g in range(3):
        landed(g, 0, sibling, 1)
        landed(g, 4, peer(3, 0, 1), 1)
        landed(g, 5, peer(1, 0, 0), 1)
        landed(g, 7, peer(3, 1, 0), 2)
        landed(g, 8, peer(1, 1, 0), 2)
        landed(g, 11, peer(2, 1, 0), 1)
        landed(g, 12, peer(2, 1, 1), 1)
        first, rows = CHUNKS[g]
        for t in range(first, first + rows, 16):
            pair = every[:, t : t + 16, :].astype(F32).reshape(NC, 2, 8, 128)
            for i in range(2):
                row = t // 8 + i
                if row == 7:
                    continue
                turned = pair[:, i].reshape(128, 128)
                x[row, :, 0:128] = (turned * gate[0]).astype(BF16)
                x[row, :, 128:256] = (turned * gate[1]).astype(BF16)
        if g == 0:
            y = dot(wz[...].reshape(128, 896), x[0:7].reshape(896, 256))
            for c in range(2):
                ob[c, 0:7] = y[64 * c : 64 * c + 56].reshape(7, 8, 256)
        else:
            w, n, lo = ((w1, 6, 8), (w2, 5, 20))[g - 1]
            flat = w[...].reshape(32 * n, 128 * n)
            plus = dot(flat, x[lo : lo + n].reshape(128 * n, 256))
            minus = dot(flat, x[lo + n : lo + 2 * n].reshape(128 * n, 256))
            for c in range(2):
                real, imag = 16 * n * c, 16 * n * c + 8 * n
                ob[c, lo - 1 : lo - 1 + n] = (
                    plus[real : real + 8 * n] - minus[imag : imag + 8 * n]
                ).reshape(n, 8, 256)
                ob[c, lo - 1 + n : lo - 1 + 2 * n] = (
                    minus[real : real + 8 * n] + plus[imag : imag + 8 * n]
                ).reshape(n, 8, 256)
    swap = remote(ob.at[other], orecv, o_send, o_recv, (space, sibling))
    swap.start()

    def turn_back(half, rows):
        for degree in range(7):
            width = 2 * degree + 1
            ahead = back = None
            for order in range(HEIGHT[degree]):
                at = OFFSET[degree] + order * width
                block = r3[half, at : at + width]
                line = rows(row_of(degree, order))
                one, two = block * line[:, :128], block * line[:, 128:]
                ahead = one if ahead is None else ahead + one
                back = two if back is None else back + two
            pf[half, degree * degree : (degree + 1) ** 2] = ahead
            pt[half, degree * degree : (degree + 1) ** 2] = back

    turn_back(core, lambda row: ob[core, row])
    swap.wait_recv()
    turn_back(other, lambda row: orecv[row])

    total = fcoef[...]
    for half in range(2):
        hi, lo = split(pf[half].reshape(392, 128))
        hot = nconst[3, :, 128 * half : 128 * half + 128]
        total = total + dot_nt(
            jnp.concatenate([hi, lo], axis=1), jnp.concatenate([hot, hot], axis=1)
        )
    hidden = total.reshape(49, 8, 128)
    lead = hidden[0]
    sigma = jax.nn.sigmoid(lead)
    energy = ewcol[0] * (lead * sigma)
    grads = [(ewcol[0] * (sigma * (1.0 + lead * (1.0 - sigma))))[None]]
    for degree in range(1, 7):
        block = hidden[degree * degree : (degree + 1) ** 2]
        square = 1.0 + jnp.sum(block * block, axis=0)
        energy = energy + ewcol[degree] * jnp.log(square)
        grads.append((ewcol[degree] * 2.0 / square) * block)
    hi, lo = split(jnp.concatenate(grads, axis=0).reshape(392, 128))
    hot = nconst[3]
    edge_grads = dot(
        jnp.concatenate([hi, lo], axis=1), jnp.concatenate([hot, hot], axis=0)
    )
    parts = []
    for half in range(2):
        block = edge_grads[:, 128 * half : 128 * half + 128].reshape(49, 8, 128)
        parts.append(jnp.sum(jnp.sum(block * pt[half], axis=0), axis=0, keepdims=True))
    parts.append(jnp.sum(energy, axis=0, keepdims=True))
    red[chan] = jnp.concatenate(parts + [jnp.zeros((5, 128), F32)], axis=0)

    def sums(d):
        to = lax.rem(chan + d, NC)
        return remote(red.at[chan], red.at[chan], r_send.at[d - 1], r_recv.at[d - 1], (space, to))

    def launch_sums(d, carry):
        sums(d).start()
        return carry

    def arrive_sums(d, carry):
        sums(d).wait_recv()
        return carry

    lax.fori_loop(1, NC, launch_sums, 0)
    lax.fori_loop(1, NC, arrive_sums, 0)
    summed = jnp.sum(red[...], axis=0)
    energy_out[...] = summed[2:3]
    pull = jnp.concatenate([summed[0:1], summed[1:2]], axis=1)
    push = jnp.concatenate([pull * u for u in unit] + [jnp.zeros((5, 256), F32)], axis=0)
    hi, lo = split(push)
    hilo = jnp.concatenate([hi.astype(F32), lo.astype(F32)], axis=0).astype(BF16)
    for side in range(2):
        part = dot_nt(hilo, nconst[1 + side])
        fsend[side] = part[0:8] + part[8:16]
    back = [
        remote(fsend.at[0], frecv.at[0], f_send.at[0], f_recv.at[0], (before, chan)),
        remote(fsend.at[1], frecv.at[1], f_send.at[1], f_recv.at[1], (after, chan)),
    ]
    for copy in back:
        copy.start()
    part = dot_nt(hilo, nconst[0]) - dot_nt(hilo, nconst[3])
    part = part[0:8] + part[8:16]
    for copy in back:
        copy.wait_recv()
    force_out[...] = (part + frecv[0] + frecv[1])[0:3]

    sent = exchange + weights + [swap] + back
    for g in range(3):
        sent = sent + own_sends(g) + [passed(g, i) for i in range(6)]
    for copy in sent:
        copy.wait_send()

    def drain(d, carry):
        sums(d).wait_send()
        return carry

    lax.fori_loop(1, NC, drain, 0)


def local(
    features, ghost_index, edge_src, edge_dst, edge_count, rotation, distance, edge_angle,
    radial_weight, conv_zero, conv_one, conv_two, energy_weight,
):
    vmem = pl.BlockSpec(memory_space=pltpu.VMEM)
    arrays = (
        features,
        ghost_index,
        edge_src.reshape(1, 256),
        edge_dst.reshape(1, 256),
        edge_count,
        rotation,
        distance.reshape(2, 128),
        edge_angle,
        radial_weight,
        conv_zero,
        conv_one,
        conv_two,
        energy_weight,
    )
    dma = pltpu.SemaphoreType.DMA
    energy, forces = pl.pallas_call(
        kernel,
        out_shape=(jax.ShapeDtypeStruct((1, 128), F32), jax.ShapeDtypeStruct((3, 128), F32)),
        in_specs=[pl.BlockSpec(memory_space=pl.ANY)] * 13,
        out_specs=(vmem, vmem),
        scratch_shapes=[(pltpu.SMEM if a.shape == (1,) else pltpu.VMEM)(a.shape, a.dtype) for a in arrays]
        + [
            pltpu.VMEM((416, 128), BF16),
            pltpu.VMEM((416, 256), F32),
            pltpu.VMEM((256, 512), BF16),
            pltpu.VMEM((2, 208, 128), BF16),
            pltpu.VMEM((8, 128), jnp.int32),
            pltpu.VMEM((2, 208, 128), BF16),
            pltpu.VMEM((2, 8, 128), jnp.int32),
            pltpu.VMEM((2, 64, 896), BF16),
            pltpu.VMEM((2, 96, 768), BF16),
            pltpu.VMEM((2, 80, 640), BF16),
            pltpu.VMEM((240, 256), F32),
            pltpu.VMEM((2, 235, 8, 128), F32),
            pltpu.VMEM((2, 49, 8, 128), F32),
            pltpu.VMEM((2, 30, 8, 128), F32),
            pltpu.VMEM((2, 240, 128), BF16),
            pltpu.VMEM((NC, 240, 128), BF16),
            pltpu.VMEM((2, 128, 128), F32),
            pltpu.VMEM((30, 128, 256), BF16),
            pltpu.VMEM((2, 29, 8, 256), F32),
            pltpu.VMEM((29, 8, 256), F32),
            pltpu.VMEM((2, 49, 8, 128), F32),
            pltpu.VMEM((2, 49, 8, 128), F32),
            pltpu.VMEM((392, 128), F32),
            pltpu.VMEM((4, 128, 256), BF16),
            pltpu.VMEM((7, 8, 128), F32),
            pltpu.VMEM((NC, 8, 128), F32),
            pltpu.VMEM((2, 8, 128), F32),
            pltpu.VMEM((2, 8, 128), F32),
            dma((4,)),
            dma((4,)),
            dma((3,)),
            dma((3,)),
            dma((13, 3)),
            dma((13, 3)),
            dma,
            dma,
            dma((NC - 1,)),
            dma((NC - 1,)),
            dma((2,)),
            dma((2,)),
            dma((13,)),
        ],
        compiler_params=pltpu.CompilerParams(
            collective_id=0, has_side_effects=True, vmem_limit_bytes=60 * 1024 * 1024
        ),
        cost_estimate=pl.CostEstimate(flops=400_000_000, bytes_accessed=3_000_000, transcendentals=200_000),
    )(*arrays)
    return (energy.reshape(128), forces)


def solution(mesh):
    in_specs = (
        P(None, "chan", "space"),
        P(None, "space"),
        P("space"),
        P("space"),
        P("space"),
        P(None, "space"),
        P("space"),
        P(None, "space"),
        P(),
        P(None, "chan", None),
        P(None, None, "chan", None),
        P(None, None, "chan", None),
        P(None, "chan"),
    )
    out_specs = (P("space"), P(None, "space"))
    return jax.shard_map(local, mesh=mesh, in_specs=in_specs, out_specs=out_specs, check_vma=False)
```

```python
import jax
import jax.numpy as jnp
from jax import lax
from jax.experimental import pallas as pl
from jax.experimental.pallas import tpu as pltpu
from jax.sharding import PartitionSpec as P

MESH = pl.DeviceIdType.MESH
F32 = jnp.float32
BF16 = jnp.bfloat16
NC = 16
CHUNKS = ((0, 64), (64, 96), (160, 80))
HEIGHT = [min(2 * l + 1, 5) for l in range(7)]
OFFSET = [sum(HEIGHT[m] * (2 * m + 1) for m in range(l)) for l in range(7)]
FIRST = (0, 7, 13, 19, 24)
LEAST = (0, 1, 1, 2, 2)
FETCH_ORDER = (9, 10, 11, 5, 2, 3, 4, 6, 8, 12, 7)


def row_of(degree, order):
    return FIRST[order] + degree - LEAST[order]


def padded_row(row):
    return row if row < 7 else row + 1


def dot(a, b):
    return jnp.dot(a, b, preferred_element_type=F32)


def dot_nt(a, b):
    return lax.dot_general(a, b, (((1,), (1,)), ((), ())), preferred_element_type=F32)


def split(x):
    hi = x.astype(BF16)
    return hi, (x - hi.astype(F32)).astype(BF16)


def kernel(*refs):
    held = refs[:13]
    energy_out, force_out = refs[13:15]
    feat, gidx, esrc, edst, count, rot, dist, ang, radial, wzero, wone, wtwo, eweight = refs[15:28]
    (
        coef, base, shot, mine, mine_g, ghost, ghost_g, wz, w1, w2, rf, r3, s3, t3, snd, every, gate, x, ob, orecv,
        pf, pt, fcoef, nconst, pushes, ewcol, red, fsend, frecv,
        g_send, g_recv, w_send, w_recv, a_send, a_recv, o_send, o_recv, r_send, r_recv, f_send, f_recv, h_recv,
    ) = refs[28:]
    fetch = [
        pltpu.make_async_copy(src, dst, h_recv.at[i])
        for i, (src, dst) in enumerate(zip(held, refs[15:28]))
    ]
    fetch[0].start()
    fetch[1].start()
    space = lax.axis_index("space")
    chan = lax.axis_index("chan")
    n_space = lax.axis_size("space")
    after = lax.rem(space + 1, n_space)
    before = lax.rem(space + n_space - 1, n_space)
    core = lax.rem(chan, 2)
    other = 1 - core
    sibling = chan + 1 - 2 * core

    def remote(src, dst, send, recv, where):
        return pltpu.make_async_remote_copy(
            src_ref=src, dst_ref=dst, send_sem=send, recv_sem=recv, device_id=where, device_id_type=MESH
        )

    barrier = pltpu.get_barrier_semaphore()

    def greet(d, carry):
        pl.semaphore_signal(barrier, inc=1, device_id=(space, lax.rem(chan + d, NC)), device_id_type=MESH)
        return carry

    pl.semaphore_signal(barrier, inc=1, device_id=(after, chan), device_id_type=MESH)
    pl.semaphore_signal(barrier, inc=1, device_id=(before, chan), device_id_type=MESH)
    lax.fori_loop(1, NC, greet, 0)
    for i in FETCH_ORDER:
        fetch[i].start()

    fetch[0].wait()
    fetch[1].wait()
    own = feat[...].astype(F32).reshape(392, 128)
    fcoef[...] = own
    own = jnp.concatenate([own, jnp.zeros((24, 128), F32)], axis=0).astype(BF16)
    coef[...] = own
    lend_row = lax.broadcasted_iota(jnp.int32, (256, 256), 0)
    lend_at = jnp.concatenate(
        [gidx[0:1, :], gidx[0:1, :] + 128, gidx[1:2, :], gidx[1:2, :] + 128], axis=1
    )
    lend_hot = (lend_at == lend_row).astype(F32).astype(BF16)
    lent = dot(jnp.concatenate([own[:208], own[208:]], axis=1), lend_hot).astype(BF16)
    mine[0] = lent[:, :128]
    mine[1] = lent[:, 128:]
    mine_g[...] = jnp.zeros((8, 128), jnp.int32)
    mine_g[0:2, 0:64] = gidx[...]
    pl.semaphore_wait(barrier, NC + 1)

    exchange = [
        remote(mine.at[0], ghost.at[0], g_send.at[0], g_recv.at[0], (after, chan)),
        remote(mine.at[1], ghost.at[1], g_send.at[0], g_recv.at[0], (before, chan)),
        remote(mine_g, ghost_g.at[0], g_send.at[1], g_recv.at[1], (after, chan)),
        remote(mine_g, ghost_g.at[1], g_send.at[1], g_recv.at[1], (before, chan)),
    ]
    both_ghosts = remote(ghost, ghost, g_send.at[0], g_recv.at[0], (after, chan))
    both_tables = remote(ghost_g, ghost_g, g_send.at[1], g_recv.at[1], (after, chan))
    for copy in exchange:
        copy.start()

    for i in (9, 10, 11):
        fetch[i].wait()
    wz[core] = jnp.concatenate(
        [wzero[...].astype(F32).reshape(56, 896), jnp.zeros((8, 896), F32)], axis=0
    ).astype(BF16)
    w1[core] = wone[...].astype(F32).reshape(96, 768).astype(BF16)
    w2[core] = wtwo[...].astype(F32).reshape(80, 640).astype(BF16)
    weights = [
        remote(w.at[core], w.at[core], w_send.at[i], w_recv.at[i], (space, sibling))
        for i, w in enumerate((wz, w1, w2))
    ]
    for copy in weights:
        copy.start()

    fetch[5].wait()
    rf[0:235, :] = rot[...].astype(F32)

    def spread(i, carry):
        for j in range(5):
            row = i * 5 + j
            line = rf[pl.ds(row, 1), :]
            r3[0, row] = jnp.broadcast_to(line[:, :128], (8, 128))
            r3[1, row] = jnp.broadcast_to(line[:, 128:], (8, 128))
        return carry

    lax.fori_loop(0, 47, spread, 0)

    for i in (2, 3, 4, 6, 7, 8, 12):
        fetch[i].wait()
    atom_row = lax.broadcasted_iota(jnp.int32, (128, 256), 0)
    source = esrc[...]
    target_hot = (edst[...] == atom_row).astype(F32)
    source_hot = (source == atom_row).astype(F32)
    nconst[0] = source_hot.astype(BF16)
    nconst[1] = target_hot.astype(BF16)
    base[...] = dot(coef[...], nconst[0])
    slot_row = lax.broadcasted_iota(jnp.int32, (256, 256), 0)
    slot_of = slot_row - 64 * (slot_row // 64) + 64 * (slot_row // 128)
    upper = (slot_row // 64) % 2
    for half in range(2):
        shot[:, 256 * half : 256 * half + 256] = (
            (source - 128 == jnp.where(upper == half, slot_of, -1000)).astype(F32).astype(BF16)
        )

    live = (lax.broadcasted_iota(jnp.int32, (1, 128), 1) + core * 128 < count[0]).astype(F32)
    center = 12.0 * lax.broadcasted_iota(jnp.int32, (512, 128), 0).astype(F32) / 511.0
    grid = dist[pl.ds(core, 1), :] - center
    basis = jnp.exp(-2.0 * grid * grid)
    slope = -4.0 * grid * basis
    both = jnp.concatenate([basis.astype(BF16), slope.astype(BF16)], axis=1)
    radial_out = lax.dot_general(
        radial[...], both, (((0,), (0,)), ((), ())), preferred_element_type=F32
    )
    preact = radial_out[:, :128]
    sigma = jax.nn.sigmoid(preact)
    gate[0] = preact * sigma * live
    gate[1] = sigma * (1.0 + preact * (1.0 - sigma)) * live * radial_out[:, 128:]

    eye = (
        lax.broadcasted_iota(jnp.int32, (8, 8), 0) == lax.broadcasted_iota(jnp.int32, (8, 8), 1)
    ).astype(F32)
    for degree in range(7):
        column = jnp.sum(eweight[degree : degree + 1, :] * eye, axis=1, keepdims=True)
        ewcol[degree] = jnp.broadcast_to(column, (8, 128))

    polar, azimuth = ang[0:1, :], ang[1:2, :]
    unit = [jnp.sin(polar) * jnp.cos(azimuth), jnp.sin(polar) * jnp.sin(azimuth), jnp.cos(polar)]

    both_ghosts.wait_recv()
    lent = dot(jnp.concatenate([ghost[0], ghost[1]], axis=1), shot[...])
    for half in range(2):
        at = 128 * half
        s3[half, 0:26] = (base[0:208, at : at + 128] + lent[:, at : at + 128]).reshape(26, 8, 128)
        s3[half, 26:49] = (
            base[208:392, at : at + 128] + lent[0:184, 256 + at : 384 + at]
        ).reshape(23, 8, 128)

    along, deep = lax.div(chan, 4), lax.rem(lax.div(chan, 2), 2)

    def peer(dy, dz, c):
        return lax.rem(along + dy, 4) * 4 + lax.rem(deep + dz, 2) * 2 + c

    def piece_of(ref, g, first, count):
        start, rows = CHUNKS[g]
        return ref.at[pl.ds(first, count), pl.ds(start, rows)]

    def blocks(g, src, dst, source, first, count, kind, to):
        return remote(
            piece_of(src, g, source, count), piece_of(dst, g, first, count), a_send, a_recv.at[kind, g], (space, to)
        )

    def own_sends(g):
        plans = [(sibling, other, 0)]
        for c in range(2):
            plans.append((peer(0, 1, c), c, 1))
        for c in range(2):
            plans.append((peer(2, 0, c), c, 2))
            plans.append((peer(1, 0, c), c, 0))
            plans.append((peer(3, 0, c), c, 0))
        return [blocks(g, snd, every, half, chan, 1, kind, to) for to, half, kind in plans]

    ahead, behind, across = peer(1, 0, core), peer(3, 0, core), peer(0, 1, core)
    paths = [
        (peer(0, 1, 0), 2, 0, ahead),
        (peer(0, 1, 0), 2, 0, behind),
        (peer(2, 0, 0), 2, 0, across),
    ]

    def passed(g, i):
        first, count, kind, to = paths[i]
        return blocks(g, every, every, first, first, count, kind, to)

    def landed(g, kind, count):
        blocks(g, every, every, 0, 0, count, kind, sibling).wait_recv()

    t3[:, 7] = jnp.zeros((2, 8, 128), F32)
    for g in range(3):
        for order in ((0,), (1, 2), (3, 4))[g]:
            for degree in range(LEAST[order], 7):
                width = 2 * degree + 1
                at = OFFSET[degree] + order * width
                row = padded_row(row_of(degree, order))
                for half in range(2):
                    t3[half, row] = jnp.sum(
                        r3[half, at : at + width] * s3[half, degree * degree : (degree + 1) ** 2], axis=0
                    )
        first, rows = CHUNKS[g]
        for half in range(2):
            snd[half, first : first + rows] = (
                t3[half, first // 8 : (first + rows) // 8].reshape(rows, 128).astype(BF16)
            )
        every[chan, first : first + rows] = snd[core, first : first + rows]

        for copy in own_sends(g):
            copy.start()

    for g in range(3):
        landed(g, 1, 2)
        passed(g, 0).start()
        passed(g, 1).start()
        landed(g, 2, 2)
        passed(g, 2).start()

    both_tables.wait_recv()
    slot_row = lax.broadcasted_iota(jnp.int32, (64, 256), 0)
    atom_lane = lax.broadcasted_iota(jnp.int32, (128, 64), 0)
    for side in range(2):
        slot_hot = (source - (128 + 64 * side) == slot_row).astype(F32).astype(BF16)
        lent_hot = (ghost_g[side, side : side + 1, 0:64] == atom_lane).astype(F32).astype(BF16)
        pushes[:, 128 * side : 128 * side + 128] = dot(lent_hot, slot_hot).T.astype(BF16)
    pushes[:, 256:384] = (nconst[0].astype(F32) - nconst[1].astype(F32)).T.astype(BF16)
    for copy in weights:
        copy.wait_recv()
    for g in range(3):
        landed(g, 0, 11)
        first, rows = CHUNKS[g]
        for t in range(first, first + rows, 16):
            pair = every[:, t : t + 16, :].astype(F32).reshape(NC, 2, 8, 128)
            for i in range(2):
                row = t // 8 + i
                if row == 7:
                    continue
                turned = pair[:, i].reshape(128, 128)
                x[row, :, 0:128] = (turned * gate[0]).astype(BF16)
                x[row, :, 128:256] = (turned * gate[1]).astype(BF16)
        if g == 0:
            y = dot(wz[...].reshape(128, 896), x[0:7].reshape(896, 256))
            for c in range(2):
                ob[c, 0:7] = y[64 * c : 64 * c + 56].reshape(7, 8, 256)
        else:
            w, n, lo = ((w1, 6, 8), (w2, 5, 20))[g - 1]
            flat = w[...].reshape(32 * n, 128 * n)
            plus = dot(flat, x[lo : lo + n].reshape(128 * n, 256))
            minus = dot(flat, x[lo + n : lo + 2 * n].reshape(128 * n, 256))
            for c in range(2):
                real, imag = 16 * n * c, 16 * n * c + 8 * n
                ob[c, lo - 1 : lo - 1 + n] = (
                    plus[real : real + 8 * n] - minus[imag : imag + 8 * n]
                ).reshape(n, 8, 256)
                ob[c, lo - 1 + n : lo - 1 + 2 * n] = (
                    minus[real : real + 8 * n] + plus[imag : imag + 8 * n]
                ).reshape(n, 8, 256)
        low, high = ((0, 7), (7, 19), (19, 29))[g]
        rows = pl.ds(low, high - low)
        remote(ob.at[other, rows], orecv.at[rows], o_send, o_recv, (space, sibling)).start()
    swap = remote(ob.at[other], orecv, o_send, o_recv, (space, sibling))

    def turn_back(half, rows):
        for degree in range(7):
            width = 2 * degree + 1
            ahead = back = None
            for order in range(HEIGHT[degree]):
                at = OFFSET[degree] + order * width
                block = r3[half, at : at + width]
                line = rows(row_of(degree, order))
                one, two = block * line[:, :128], block * line[:, 128:]
                ahead = one if ahead is None else ahead + one
                back = two if back is None else back + two
            pf[half, degree * degree : (degree + 1) ** 2] = ahead
            pt[half, degree * degree : (degree + 1) ** 2] = back

    turn_back(core, lambda row: ob[core, row])
    swap.wait_recv()
    turn_back(other, lambda row: orecv[row])

    total = fcoef[...]
    for half in range(2):
        hi, lo = split(pf[half].reshape(392, 128))
        hot = nconst[1, :, 128 * half : 128 * half + 128]
        total = total + dot_nt(
            jnp.concatenate([hi, lo], axis=1), jnp.concatenate([hot, hot], axis=1)
        )
    hidden = total.reshape(49, 8, 128)
    lead = hidden[0]
    sigma = jax.nn.sigmoid(lead)
    energy = ewcol[0] * (lead * sigma)
    grads = [(ewcol[0] * (sigma * (1.0 + lead * (1.0 - sigma))))[None]]
    for degree in range(1, 7):
        block = hidden[degree * degree : (degree + 1) ** 2]
        square = 1.0 + jnp.sum(block * block, axis=0)
        energy = energy + ewcol[degree] * jnp.log(square)
        grads.append((ewcol[degree] * 2.0 / square) * block)
    hi, lo = split(jnp.concatenate(grads, axis=0).reshape(392, 128))
    hot = nconst[1]
    edge_grads = dot(
        jnp.concatenate([hi, lo], axis=1), jnp.concatenate([hot, hot], axis=0)
    )
    parts = []
    for half in range(2):
        block = edge_grads[:, 128 * half : 128 * half + 128].reshape(49, 8, 128)
        parts.append(jnp.sum(jnp.sum(block * pt[half], axis=0), axis=0, keepdims=True))
    parts.append(jnp.sum(energy, axis=0, keepdims=True))
    red[chan] = jnp.concatenate(parts + [jnp.zeros((5, 128), F32)], axis=0)

    def sums(d):
        to = lax.rem(chan + d, NC)
        return remote(red.at[chan], red.at[chan], r_send, r_recv, (space, to))

    def launch_sums(d, carry):
        sums(d).start()
        return carry

    all_sums = remote(red.at[pl.ds(0, NC - 1)], red.at[pl.ds(0, NC - 1)], r_send, r_recv, (space, sibling))
    lax.fori_loop(1, NC, launch_sums, 0)
    both_ghosts.wait_send()
    both_tables.wait_send()
    for copy in weights + [swap]:
        copy.wait_send()
    whole = every.at[pl.ds(0, NC - 1)]
    remote(whole, whole, a_send, a_recv.at[0, 0], (space, sibling)).wait_send()
    all_sums.wait_recv()
    summed = jnp.sum(red[...], axis=0)
    energy_out[...] = summed[2:3]
    pull = jnp.concatenate([summed[0:1], summed[1:2]], axis=1)
    push = jnp.concatenate([pull * u for u in unit] + [jnp.zeros((5, 256), F32)], axis=0)
    hi, lo = split(push)
    hilo = jnp.concatenate([hi.astype(F32), lo.astype(F32)], axis=0).astype(BF16)
    part = dot(hilo, pushes[...])
    part = part[0:8] + part[8:16]
    fsend[0] = part[:, 0:128]
    fsend[1] = part[:, 128:256]
    back = [
        remote(fsend.at[0], frecv.at[0], f_send, f_recv, (before, chan)),
        remote(fsend.at[1], frecv.at[1], f_send, f_recv, (after, chan)),
    ]
    for copy in back:
        copy.start()
    both_back = remote(fsend, frecv, f_send, f_recv, (before, chan))
    all_sums.wait_send()
    both_back.wait_recv()
    force_out[...] = (part[:, 256:384] + frecv[0] + frecv[1])[0:3]

    both_back.wait_send()


def local(
    features, ghost_index, edge_src, edge_dst, edge_count, rotation, distance, edge_angle,
    radial_weight, conv_zero, conv_one, conv_two, energy_weight,
):
    vmem = pl.BlockSpec(memory_space=pltpu.VMEM)
    arrays = (
        features,
        ghost_index,
        edge_src.reshape(1, 256),
        edge_dst.reshape(1, 256),
        edge_count,
        rotation,
        distance.reshape(2, 128),
        edge_angle,
        radial_weight,
        conv_zero,
        conv_one,
        conv_two,
        energy_weight,
    )
    dma = pltpu.SemaphoreType.DMA
    energy, forces = pl.pallas_call(
        kernel,
        out_shape=(jax.ShapeDtypeStruct((1, 128), F32), jax.ShapeDtypeStruct((3, 128), F32)),
        in_specs=[pl.BlockSpec(memory_space=pl.ANY)] * 13,
        out_specs=(vmem, vmem),
        scratch_shapes=[(pltpu.SMEM if a.shape == (1,) else pltpu.VMEM)(a.shape, a.dtype) for a in arrays]
        + [
            pltpu.VMEM((416, 128), BF16),
            pltpu.VMEM((416, 256), F32),
            pltpu.VMEM((256, 512), BF16),
            pltpu.VMEM((2, 208, 128), BF16),
            pltpu.VMEM((8, 128), jnp.int32),
            pltpu.VMEM((2, 208, 128), BF16),
            pltpu.VMEM((2, 8, 128), jnp.int32),
            pltpu.VMEM((2, 64, 896), BF16),
            pltpu.VMEM((2, 96, 768), BF16),
            pltpu.VMEM((2, 80, 640), BF16),
            pltpu.VMEM((240, 256), F32),
            pltpu.VMEM((2, 235, 8, 128), F32),
            pltpu.VMEM((2, 49, 8, 128), F32),
            pltpu.VMEM((2, 30, 8, 128), F32),
            pltpu.VMEM((2, 240, 128), BF16),
            pltpu.VMEM((NC, 240, 128), BF16),
            pltpu.VMEM((2, 128, 128), F32),
            pltpu.VMEM((30, 128, 256), BF16),
            pltpu.VMEM((2, 29, 8, 256), F32),
            pltpu.VMEM((29, 8, 256), F32),
            pltpu.VMEM((2, 49, 8, 128), F32),
            pltpu.VMEM((2, 49, 8, 128), F32),
            pltpu.VMEM((392, 128), F32),
            pltpu.VMEM((2, 128, 256), BF16),
            pltpu.VMEM((256, 384), BF16),
            pltpu.VMEM((7, 8, 128), F32),
            pltpu.VMEM((NC, 8, 128), F32),
            pltpu.VMEM((2, 8, 128), F32),
            pltpu.VMEM((2, 8, 128), F32),
            dma((2,)),
            dma((2,)),
            dma((3,)),
            dma((3,)),
            dma,
            dma((3, 3)),
            dma,
            dma,
            dma,
            dma,
            dma,
            dma,
            dma((13,)),
        ],
        compiler_params=pltpu.CompilerParams(
            collective_id=0, has_side_effects=True, vmem_limit_bytes=60 * 1024 * 1024
        ),
        cost_estimate=pl.CostEstimate(flops=400_000_000, bytes_accessed=3_000_000, transcendentals=200_000),
    )(*arrays)
    return (energy.reshape(128), forces)


def solution(mesh):
    in_specs = (
        P(None, "chan", "space"),
        P(None, "space"),
        P("space"),
        P("space"),
        P("space"),
        P(None, "space"),
        P("space"),
        P(None, "space"),
        P(),
        P(None, "chan", None),
        P(None, None, "chan", None),
        P(None, None, "chan", None),
        P(None, "chan"),
    )
    out_specs = (P("space"), P(None, "space"))
    return jax.shard_map(local, mesh=mesh, in_specs=in_specs, out_specs=out_specs, check_vma=False)
```

```python
import jax
import jax.numpy as jnp
from jax import lax
from jax.experimental import pallas as pl
from jax.experimental.pallas import tpu as pltpu
from jax.sharding import PartitionSpec as P

MESH = pl.DeviceIdType.MESH
F32 = jnp.float32
BF16 = jnp.bfloat16
NC = 16
CHUNKS = ((0, 64), (64, 96), (160, 80))
HEIGHT = [min(2 * l + 1, 5) for l in range(7)]
OFFSET = [sum(HEIGHT[m] * (2 * m + 1) for m in range(l)) for l in range(7)]
FIRST = (0, 7, 13, 19, 24)
LEAST = (0, 1, 1, 2, 2)
FETCH_ORDER = (9, 10, 11, 5, 2, 3, 4, 6, 8, 12, 7)


def row_of(degree, order):
    return FIRST[order] + degree - LEAST[order]


def padded_row(row):
    return row if row < 7 else row + 1


def dot(a, b):
    return jnp.dot(a, b, preferred_element_type=F32)


def dot_nt(a, b):
    return lax.dot_general(a, b, (((1,), (1,)), ((), ())), preferred_element_type=F32)


def split(x):
    hi = x.astype(BF16)
    return hi, (x - hi.astype(F32)).astype(BF16)


def kernel(*refs):
    held = refs[:13]
    energy_out, force_out = refs[13:15]
    feat, gidx, esrc, edst, count, rot, dist, ang, radial, wzero, wone, wtwo, eweight = refs[15:28]
    (
        coef, base, shot, mine, mine_g, ghost, ghost_g, wz, w1, w2, rf, r3, s3, t3, snd, every, gate, x, ob, orecv,
        pf, pt, fcoef, nconst, pushes, ewcol, red, fsend, frecv, fsum,
        g_send, g_recv, w_send, w_recv, a_send, a_recv, o_send, o_recv, r_send, r_recv, f_send, f_recv, h_recv,
    ) = refs[28:]
    fetch = [
        pltpu.make_async_copy(src, dst, h_recv.at[i])
        for i, (src, dst) in enumerate(zip(held, refs[15:28]))
    ]
    fetch[0].start()
    fetch[1].start()
    space = lax.axis_index("space")
    chan = lax.axis_index("chan")
    n_space = lax.axis_size("space")
    after = lax.rem(space + 1, n_space)
    before = lax.rem(space + n_space - 1, n_space)
    core = lax.rem(chan, 2)
    other = 1 - core
    sibling = chan + 1 - 2 * core

    def remote(src, dst, send, recv, where):
        return pltpu.make_async_remote_copy(
            src_ref=src, dst_ref=dst, send_sem=send, recv_sem=recv, device_id=where, device_id_type=MESH
        )

    along, deep = lax.div(chan, 4), lax.rem(lax.div(chan, 2), 2)

    def peer(dy, dz, c):
        return lax.rem(along + dy, 4) * 4 + lax.rem(deep + dz, 2) * 2 + c

    chip = lax.div(chan, 2)
    barrier = pltpu.get_barrier_semaphore()

    def greet(where):
        pl.semaphore_signal(barrier, inc=1, device_id=where, device_id_type=MESH)

    greet((after, chan))
    greet((before, chan))
    greet((space, sibling))
    for c in range(2):
        for dy, dz in ((0, 1), (1, 0), (3, 0), (2, 0)):
            greet((space, peer(dy, dz, c)))
    for dy in range(1, 4):
        greet((space, peer(dy, 1, core)))
    for i in FETCH_ORDER:
        fetch[i].start()

    fetch[0].wait()
    fetch[1].wait()
    own = feat[...].astype(F32).reshape(392, 128)
    fcoef[...] = own
    own = jnp.concatenate([own, jnp.zeros((24, 128), F32)], axis=0).astype(BF16)
    coef[...] = own
    lend_row = lax.broadcasted_iota(jnp.int32, (256, 256), 0)
    lend_at = jnp.concatenate(
        [gidx[0:1, :], gidx[0:1, :] + 128, gidx[1:2, :], gidx[1:2, :] + 128], axis=1
    )
    lend_hot = (lend_at == lend_row).astype(F32).astype(BF16)
    lent = dot(jnp.concatenate([own[:208], own[208:]], axis=1), lend_hot).astype(BF16)
    mine[0] = lent[:, :128]
    mine[1] = lent[:, 128:]
    mine_g[...] = jnp.zeros((8, 128), jnp.int32)
    mine_g[0:2, 0:64] = gidx[...]
    pl.semaphore_wait(barrier, 14)

    exchange = [
        remote(mine.at[0], ghost.at[0], g_send.at[0], g_recv.at[0], (after, chan)),
        remote(mine.at[1], ghost.at[1], g_send.at[0], g_recv.at[0], (before, chan)),
        remote(mine_g, ghost_g.at[0], g_send.at[1], g_recv.at[1], (after, chan)),
        remote(mine_g, ghost_g.at[1], g_send.at[1], g_recv.at[1], (before, chan)),
    ]
    both_ghosts = remote(ghost, ghost, g_send.at[0], g_recv.at[0], (after, chan))
    both_tables = remote(ghost_g, ghost_g, g_send.at[1], g_recv.at[1], (after, chan))
    for copy in exchange:
        copy.start()

    for i in (9, 10, 11):
        fetch[i].wait()
    wz[core] = jnp.concatenate(
        [wzero[...].astype(F32).reshape(56, 896), jnp.zeros((8, 896), F32)], axis=0
    ).astype(BF16)
    w1[core] = wone[...].astype(F32).reshape(96, 768).astype(BF16)
    w2[core] = wtwo[...].astype(F32).reshape(80, 640).astype(BF16)
    weights = [
        remote(w.at[core], w.at[core], w_send.at[i], w_recv.at[i], (space, sibling))
        for i, w in enumerate((wz, w1, w2))
    ]
    for copy in weights:
        copy.start()

    fetch[5].wait()
    rf[0:235, :] = rot[...].astype(F32)

    def spread(i, carry):
        for j in range(5):
            row = i * 5 + j
            line = rf[pl.ds(row, 1), :]
            r3[0, row] = jnp.broadcast_to(line[:, :128], (8, 128))
            r3[1, row] = jnp.broadcast_to(line[:, 128:], (8, 128))
        return carry

    lax.fori_loop(0, 47, spread, 0)

    for i in (2, 3, 4, 6, 7, 8, 12):
        fetch[i].wait()
    atom_row = lax.broadcasted_iota(jnp.int32, (128, 256), 0)
    source = esrc[...]
    target_hot = (edst[...] == atom_row).astype(F32)
    source_hot = (source == atom_row).astype(F32)
    nconst[0] = source_hot.astype(BF16)
    nconst[1] = target_hot.astype(BF16)
    base[...] = dot(coef[...], nconst[0])
    slot_row = lax.broadcasted_iota(jnp.int32, (256, 256), 0)
    slot_of = slot_row - 64 * (slot_row // 64) + 64 * (slot_row // 128)
    upper = (slot_row // 64) % 2
    for half in range(2):
        shot[:, 256 * half : 256 * half + 256] = (
            (source - 128 == jnp.where(upper == half, slot_of, -1000)).astype(F32).astype(BF16)
        )

    live = (lax.broadcasted_iota(jnp.int32, (1, 128), 1) + core * 128 < count[0]).astype(F32)
    center = 12.0 * lax.broadcasted_iota(jnp.int32, (512, 128), 0).astype(F32) / 511.0
    grid = dist[pl.ds(core, 1), :] - center
    basis = jnp.exp(-2.0 * grid * grid)
    slope = -4.0 * grid * basis
    both = jnp.concatenate([basis.astype(BF16), slope.astype(BF16)], axis=1)
    radial_out = lax.dot_general(
        radial[...], both, (((0,), (0,)), ((), ())), preferred_element_type=F32
    )
    preact = radial_out[:, :128]
    sigma = jax.nn.sigmoid(preact)
    gate[0] = preact * sigma * live
    gate[1] = sigma * (1.0 + preact * (1.0 - sigma)) * live * radial_out[:, 128:]

    eye = (
        lax.broadcasted_iota(jnp.int32, (8, 8), 0) == lax.broadcasted_iota(jnp.int32, (8, 8), 1)
    ).astype(F32)
    for degree in range(7):
        column = jnp.sum(eweight[degree : degree + 1, :] * eye, axis=1, keepdims=True)
        ewcol[degree] = jnp.broadcast_to(column, (8, 128))

    polar, azimuth = ang[0:1, :], ang[1:2, :]
    unit = [jnp.sin(polar) * jnp.cos(azimuth), jnp.sin(polar) * jnp.sin(azimuth), jnp.cos(polar)]

    both_ghosts.wait_recv()
    lent = dot(jnp.concatenate([ghost[0], ghost[1]], axis=1), shot[...])
    for half in range(2):
        at = 128 * half
        s3[half, 0:26] = (base[0:208, at : at + 128] + lent[:, at : at + 128]).reshape(26, 8, 128)
        s3[half, 26:49] = (
            base[208:392, at : at + 128] + lent[0:184, 256 + at : 384 + at]
        ).reshape(23, 8, 128)

    def piece_of(ref, g, first, count):
        start, rows = CHUNKS[g]
        return ref.at[pl.ds(first, count), pl.ds(start, rows)]

    def blocks(g, src, dst, source, first, count, kind, to):
        return remote(
            piece_of(src, g, source, count), piece_of(dst, g, first, count), a_send, a_recv.at[kind, g], (space, to)
        )

    def own_sends(g):
        plans = [(sibling, other, 0)]
        for c in range(2):
            plans.append((peer(0, 1, c), c, 1))
        for c in range(2):
            plans.append((peer(2, 0, c), c, 2))
            plans.append((peer(1, 0, c), c, 0))
            plans.append((peer(3, 0, c), c, 0))
        return [blocks(g, snd, every, half, chan, 1, kind, to) for to, half, kind in plans]

    ahead, behind, across = peer(1, 0, core), peer(3, 0, core), peer(0, 1, core)
    paths = [
        (peer(0, 1, 0), 2, 0, ahead),
        (peer(0, 1, 0), 2, 0, behind),
        (peer(2, 0, 0), 2, 0, across),
    ]

    def passed(g, i):
        first, count, kind, to = paths[i]
        return blocks(g, every, every, first, first, count, kind, to)

    def landed(g, kind, count):
        blocks(g, every, every, 0, 0, count, kind, sibling).wait_recv()

    t3[:, 7] = jnp.zeros((2, 8, 128), F32)
    for g in (1, 2, 0):
        for order in ((0,), (1, 2), (3, 4))[g]:
            for degree in range(LEAST[order], 7):
                width = 2 * degree + 1
                at = OFFSET[degree] + order * width
                row = padded_row(row_of(degree, order))
                for half in range(2):
                    t3[half, row] = jnp.sum(
                        r3[half, at : at + width] * s3[half, degree * degree : (degree + 1) ** 2], axis=0
                    )
        first, rows = CHUNKS[g]
        for half in range(2):
            snd[half, first : first + rows] = (
                t3[half, first // 8 : (first + rows) // 8].reshape(rows, 128).astype(BF16)
            )
        every[chan, first : first + rows] = snd[core, first : first + rows]

        for copy in own_sends(g):
            copy.start()

    for g in (1, 2, 0):
        landed(g, 1, 2)
        passed(g, 0).start()
        passed(g, 1).start()
        landed(g, 2, 2)
        passed(g, 2).start()

    both_tables.wait_recv()
    slot_row = lax.broadcasted_iota(jnp.int32, (64, 256), 0)
    atom_lane = lax.broadcasted_iota(jnp.int32, (128, 64), 0)
    for side in range(2):
        slot_hot = (source - (128 + 64 * side) == slot_row).astype(F32).astype(BF16)
        lent_hot = (ghost_g[side, side : side + 1, 0:64] == atom_lane).astype(F32).astype(BF16)
        pushes[:, 128 * side : 128 * side + 128] = dot(lent_hot, slot_hot).T.astype(BF16)
    pushes[:, 256:384] = (nconst[0].astype(F32) - nconst[1].astype(F32)).T.astype(BF16)
    for copy in weights:
        copy.wait_recv()
    for g in (1, 2, 0):
        landed(g, 0, 11)
        first, rows = CHUNKS[g]
        for t in range(first, first + rows, 16):
            pair = every[:, t : t + 16, :].astype(F32).reshape(NC, 2, 8, 128)
            for i in range(2):
                row = t // 8 + i
                if row == 7:
                    continue
                turned = pair[:, i].reshape(128, 128)
                x[row, :, 0:128] = (turned * gate[0]).astype(BF16)
                x[row, :, 128:256] = (turned * gate[1]).astype(BF16)
        if g == 0:
            y = dot(wz[...].reshape(128, 896), x[0:7].reshape(896, 256))
            for c in range(2):
                ob[c, 0:7] = y[64 * c : 64 * c + 56].reshape(7, 8, 256)
        else:
            w, n, lo = ((w1, 6, 8), (w2, 5, 20))[g - 1]
            flat = w[...].reshape(32 * n, 128 * n)
            plus = dot(flat, x[lo : lo + n].reshape(128 * n, 256))
            minus = dot(flat, x[lo + n : lo + 2 * n].reshape(128 * n, 256))
            for c in range(2):
                real, imag = 16 * n * c, 16 * n * c + 8 * n
                ob[c, lo - 1 : lo - 1 + n] = (
                    plus[real : real + 8 * n] - minus[imag : imag + 8 * n]
                ).reshape(n, 8, 256)
                ob[c, lo - 1 + n : lo - 1 + 2 * n] = (
                    minus[real : real + 8 * n] + plus[imag : imag + 8 * n]
                ).reshape(n, 8, 256)
        low, high = ((0, 7), (7, 19), (19, 29))[g]
        rows = pl.ds(low, high - low)
        remote(ob.at[other, rows], orecv.at[rows], o_send, o_recv, (space, sibling)).start()
    swap = remote(ob.at[other], orecv, o_send, o_recv, (space, sibling))

    def turn_back(half, rows):
        for degree in range(7):
            width = 2 * degree + 1
            ahead = back = None
            for order in range(HEIGHT[degree]):
                at = OFFSET[degree] + order * width
                block = r3[half, at : at + width]
                line = rows(row_of(degree, order))
                one, two = block * line[:, :128], block * line[:, 128:]
                ahead = one if ahead is None else ahead + one
                back = two if back is None else back + two
            pf[half, degree * degree : (degree + 1) ** 2] = ahead
            pt[half, degree * degree : (degree + 1) ** 2] = back

    turn_back(core, lambda row: ob[core, row])
    swap.wait_recv()
    turn_back(other, lambda row: orecv[row])

    total = fcoef[...]
    for half in range(2):
        hi, lo = split(pf[half].reshape(392, 128))
        hot = nconst[1, :, 128 * half : 128 * half + 128]
        total = total + dot_nt(
            jnp.concatenate([hi, lo], axis=1), jnp.concatenate([hot, hot], axis=1)
        )
    hidden = total.reshape(49, 8, 128)
    lead = hidden[0]
    sigma = jax.nn.sigmoid(lead)
    energy = ewcol[0] * (lead * sigma)
    grads = [(ewcol[0] * (sigma * (1.0 + lead * (1.0 - sigma))))[None]]
    for degree in range(1, 7):
        block = hidden[degree * degree : (degree + 1) ** 2]
        square = 1.0 + jnp.sum(block * block, axis=0)
        energy = energy + ewcol[degree] * jnp.log(square)
        grads.append((ewcol[degree] * 2.0 / square) * block)
    hi, lo = split(jnp.concatenate(grads, axis=0).reshape(392, 128))
    hot = nconst[1]
    edge_grads = dot(
        jnp.concatenate([hi, lo], axis=1), jnp.concatenate([hot, hot], axis=0)
    )
    parts = []
    for half in range(2):
        block = edge_grads[:, 128 * half : 128 * half + 128].reshape(49, 8, 128)
        parts.append(jnp.sum(jnp.sum(block * pt[half], axis=0), axis=0, keepdims=True))
    parts.append(jnp.sum(energy, axis=0, keepdims=True))
    pull = jnp.concatenate(parts[:2], axis=1)
    push = jnp.concatenate([pull * u for u in unit] + [jnp.zeros((5, 256), F32)], axis=0)
    hi, lo = split(push)
    hilo = jnp.concatenate([hi.astype(F32), lo.astype(F32)], axis=0).astype(BF16)
    part = dot(hilo, pushes[...])
    part = part[0:8] + part[8:16]
    rank = lax.broadcasted_iota(jnp.int32, (8, 128), 0)
    fsend[0] = part[:, 0:128]
    fsend[1] = part[:, 128:256]
    fsend[2] = jnp.where(rank == 3, parts[2], part[:, 256:384])
    halves = remote(fsend, frecv, f_send, f_recv, (space, sibling))
    halves.start()
    both_ghosts.wait_send()
    both_tables.wait_send()
    for copy in weights + [swap]:
        copy.wait_send()
    whole = every.at[pl.ds(0, NC - 1)]
    remote(whole, whole, a_send, a_recv.at[0, 0], (space, sibling)).wait_send()
    halves.wait_recv()
    fsum[...] = fsend[...] + frecv[...]
    red[chip] = fsum[2]

    def deliver(side, slot, where):
        remote(fsum.at[side], red.at[slot], r_send, r_recv, where).start()

    for d in range(8):
        to = lax.rem(chip + 4 + d, 8) * 2 + core
        deliver(0, 8 + chip, (before, to))
        deliver(1, 16 + chip, (after, to))
    for d in (4, 3, 5, 2, 6, 1, 7):
        deliver(2, chip, (space, lax.rem(chip + d, 8) * 2 + core))
    most = red.at[pl.ds(0, 23)]
    all_sums = remote(most, most, r_send, r_recv, (space, sibling))
    all_sums.wait_recv()
    summed = jnp.sum(red[...], axis=0)
    energy_out[...] = summed[3:4]
    force_out[...] = summed[0:3]
    halves.wait_send()
    all_sums.wait_send()


def local(
    features, ghost_index, edge_src, edge_dst, edge_count, rotation, distance, edge_angle,
    radial_weight, conv_zero, conv_one, conv_two, energy_weight,
):
    vmem = pl.BlockSpec(memory_space=pltpu.VMEM)
    arrays = (
        features,
        ghost_index,
        edge_src.reshape(1, 256),
        edge_dst.reshape(1, 256),
        edge_count,
        rotation,
        distance.reshape(2, 128),
        edge_angle,
        radial_weight,
        conv_zero,
        conv_one,
        conv_two,
        energy_weight,
    )
    dma = pltpu.SemaphoreType.DMA
    energy, forces = pl.pallas_call(
        kernel,
        out_shape=(jax.ShapeDtypeStruct((1, 128), F32), jax.ShapeDtypeStruct((3, 128), F32)),
        in_specs=[pl.BlockSpec(memory_space=pl.ANY)] * 13,
        out_specs=(vmem, vmem),
        scratch_shapes=[(pltpu.SMEM if a.shape == (1,) else pltpu.VMEM)(a.shape, a.dtype) for a in arrays]
        + [
            pltpu.VMEM((416, 128), BF16),
            pltpu.VMEM((416, 256), F32),
            pltpu.VMEM((256, 512), BF16),
            pltpu.VMEM((2, 208, 128), BF16),
            pltpu.VMEM((8, 128), jnp.int32),
            pltpu.VMEM((2, 208, 128), BF16),
            pltpu.VMEM((2, 8, 128), jnp.int32),
            pltpu.VMEM((2, 64, 896), BF16),
            pltpu.VMEM((2, 96, 768), BF16),
            pltpu.VMEM((2, 80, 640), BF16),
            pltpu.VMEM((240, 256), F32),
            pltpu.VMEM((2, 235, 8, 128), F32),
            pltpu.VMEM((2, 49, 8, 128), F32),
            pltpu.VMEM((2, 30, 8, 128), F32),
            pltpu.VMEM((2, 240, 128), BF16),
            pltpu.VMEM((NC, 240, 128), BF16),
            pltpu.VMEM((2, 128, 128), F32),
            pltpu.VMEM((30, 128, 256), BF16),
            pltpu.VMEM((2, 29, 8, 256), F32),
            pltpu.VMEM((29, 8, 256), F32),
            pltpu.VMEM((2, 49, 8, 128), F32),
            pltpu.VMEM((2, 49, 8, 128), F32),
            pltpu.VMEM((392, 128), F32),
            pltpu.VMEM((2, 128, 256), BF16),
            pltpu.VMEM((256, 384), BF16),
            pltpu.VMEM((7, 8, 128), F32),
            pltpu.VMEM((24, 8, 128), F32),
            pltpu.VMEM((3, 8, 128), F32),
            pltpu.VMEM((3, 8, 128), F32),
            pltpu.VMEM((3, 8, 128), F32),
            dma((2,)),
            dma((2,)),
            dma((3,)),
            dma((3,)),
            dma,
            dma((3, 3)),
            dma,
            dma,
            dma,
            dma,
            dma,
            dma,
            dma((13,)),
        ],
        compiler_params=pltpu.CompilerParams(
            collective_id=0, has_side_effects=True, vmem_limit_bytes=60 * 1024 * 1024
        ),
        cost_estimate=pl.CostEstimate(flops=400_000_000, bytes_accessed=3_000_000, transcendentals=200_000),
    )(*arrays)
    return (energy.reshape(128), forces)


def solution(mesh):
    in_specs = (
        P(None, "chan", "space"),
        P(None, "space"),
        P("space"),
        P("space"),
        P("space"),
        P(None, "space"),
        P("space"),
        P(None, "space"),
        P(),
        P(None, "chan", None),
        P(None, None, "chan", None),
        P(None, None, "chan", None),
        P(None, "chan"),
    )
    out_specs = (P("space"), P(None, "space"))
    return jax.shard_map(local, mesh=mesh, in_specs=in_specs, out_specs=out_specs, check_vma=False)
```

```python
import jax
import jax.numpy as jnp
from jax import lax
from jax.experimental import pallas as pl
from jax.experimental.pallas import tpu as pltpu
from jax.sharding import PartitionSpec as P

MESH = pl.DeviceIdType.MESH
F32 = jnp.float32
BF16 = jnp.bfloat16
NC = 16
CHUNKS = ((0, 64), (64, 96), (160, 80))
HEIGHT = [min(2 * l + 1, 5) for l in range(7)]
OFFSET = [sum(HEIGHT[m] * (2 * m + 1) for m in range(l)) for l in range(7)]
FIRST = (0, 7, 13, 19, 24)
LEAST = (0, 1, 1, 2, 2)
FETCH_ORDER = (9, 10, 11, 5, 2, 3, 4, 6, 8, 12, 7)


def row_of(degree, order):
    return FIRST[order] + degree - LEAST[order]


def padded_row(row):
    return row if row < 7 else row + 1


def dot(a, b):
    return jnp.dot(a, b, preferred_element_type=F32)


def dot_nt(a, b):
    return lax.dot_general(a, b, (((1,), (1,)), ((), ())), preferred_element_type=F32)


def split(x):
    hi = x.astype(BF16)
    return hi, (x - hi.astype(F32)).astype(BF16)


def kernel(*refs):
    held = refs[:13]
    energy_out, force_out = refs[13:15]
    feat, gidx, esrc, edst, count, rot, dist, ang, radial, wzero, wone, wtwo, eweight = refs[15:28]
    (
        coef, base, shot, mine, mine_g, ghost, ghost_g, wz, w1, w2, rf, r3, s3, t3, snd, every, gate, x, ob, orecv,
        pf, pt, fcoef, nconst, pushes, ewcol, red, fsend, frecv, fsum,
        g_send, g_recv, w_send, w_recv, a_send, a_recv, o_send, o_recv, r_send, r_recv, f_send, f_recv, h_recv,
    ) = refs[28:]
    fetch = [
        pltpu.make_async_copy(src, dst, h_recv.at[i])
        for i, (src, dst) in enumerate(zip(held, refs[15:28]))
    ]
    fetch[0].start()
    fetch[1].start()
    space = lax.axis_index("space")
    chan = lax.axis_index("chan")
    n_space = lax.axis_size("space")
    after = lax.rem(space + 1, n_space)
    before = lax.rem(space + n_space - 1, n_space)
    core = lax.rem(chan, 2)
    other = 1 - core
    sibling = chan + 1 - 2 * core

    def remote(src, dst, send, recv, where):
        return pltpu.make_async_remote_copy(
            src_ref=src, dst_ref=dst, send_sem=send, recv_sem=recv, device_id=where, device_id_type=MESH
        )

    along, deep = lax.div(chan, 4), lax.rem(lax.div(chan, 2), 2)

    def peer(dy, dz, c):
        return lax.rem(along + dy, 4) * 4 + lax.rem(deep + dz, 2) * 2 + c

    chip = lax.div(chan, 2)
    barrier = pltpu.get_barrier_semaphore()

    def greet(where):
        pl.semaphore_signal(barrier, inc=1, device_id=where, device_id_type=MESH)

    greet((after, chan))
    greet((before, chan))
    greet((space, sibling))
    for c in range(2):
        for dy, dz in ((0, 1), (1, 0), (3, 0), (2, 0)):
            greet((space, peer(dy, dz, c)))
    for dy in range(1, 4):
        greet((space, peer(dy, 1, core)))
    for i in FETCH_ORDER:
        fetch[i].start()

    fetch[0].wait()
    fetch[1].wait()
    own = feat[...].astype(F32).reshape(392, 128)
    fcoef[...] = own
    own = jnp.concatenate([own, jnp.zeros((24, 128), F32)], axis=0).astype(BF16)
    coef[...] = own
    lend_row = lax.broadcasted_iota(jnp.int32, (256, 256), 0)
    lend_at = jnp.concatenate(
        [gidx[0:1, :], gidx[0:1, :] + 128, gidx[1:2, :], gidx[1:2, :] + 128], axis=1
    )
    lend_hot = (lend_at == lend_row).astype(F32).astype(BF16)
    lent = dot(jnp.concatenate([own[:208], own[208:]], axis=1), lend_hot).astype(BF16)
    mine[0] = lent[:, :128]
    mine[1] = lent[:, 128:]
    mine_g[...] = jnp.zeros((8, 128), jnp.int32)
    mine_g[0:2, 0:64] = gidx[...]
    pl.semaphore_wait(barrier, 14)

    exchange = [
        remote(mine.at[0], ghost.at[0], g_send.at[0], g_recv.at[0], (after, chan)),
        remote(mine.at[1], ghost.at[1], g_send.at[0], g_recv.at[0], (before, chan)),
        remote(mine_g, ghost_g.at[0], g_send.at[1], g_recv.at[1], (after, chan)),
        remote(mine_g, ghost_g.at[1], g_send.at[1], g_recv.at[1], (before, chan)),
    ]
    both_ghosts = remote(ghost, ghost, g_send.at[0], g_recv.at[0], (after, chan))
    both_tables = remote(ghost_g, ghost_g, g_send.at[1], g_recv.at[1], (after, chan))
    for copy in exchange:
        copy.start()

    for i in (9, 10, 11):
        fetch[i].wait()
    wz[core] = jnp.concatenate(
        [wzero[...].astype(F32).reshape(56, 896), jnp.zeros((8, 896), F32)], axis=0
    ).astype(BF16)
    w1[core] = wone[...].astype(F32).reshape(96, 768).astype(BF16)
    w2[core] = wtwo[...].astype(F32).reshape(80, 640).astype(BF16)
    weights = [
        remote(w.at[core], w.at[core], w_send.at[i], w_recv.at[i], (space, sibling))
        for i, w in enumerate((wz, w1, w2))
    ]
    for copy in weights:
        copy.start()

    fetch[5].wait()
    rf[0:235, :] = rot[...].astype(F32)

    def spread(i, carry):
        for j in range(5):
            row = i * 5 + j
            line = rf[pl.ds(row, 1), :]
            r3[0, row] = jnp.broadcast_to(line[:, :128], (8, 128))
            r3[1, row] = jnp.broadcast_to(line[:, 128:], (8, 128))
        return carry

    lax.fori_loop(0, 47, spread, 0)

    for i in (2, 3, 4, 6, 7, 8, 12):
        fetch[i].wait()
    atom_row = lax.broadcasted_iota(jnp.int32, (128, 256), 0)
    source = esrc[...]
    target_hot = (edst[...] == atom_row).astype(F32)
    source_hot = (source == atom_row).astype(F32)
    nconst[0] = source_hot.astype(BF16)
    nconst[1] = target_hot.astype(BF16)
    base[...] = dot(coef[...], nconst[0])
    slot_row = lax.broadcasted_iota(jnp.int32, (256, 256), 0)
    slot_of = slot_row - 64 * (slot_row // 64) + 64 * (slot_row // 128)
    upper = (slot_row // 64) % 2
    for half in range(2):
        shot[:, 256 * half : 256 * half + 256] = (
            (source - 128 == jnp.where(upper == half, slot_of, -1000)).astype(F32).astype(BF16)
        )

    live = (lax.broadcasted_iota(jnp.int32, (1, 128), 1) + core * 128 < count[0]).astype(F32)
    center = 12.0 * lax.broadcasted_iota(jnp.int32, (512, 128), 0).astype(F32) / 511.0
    grid = dist[pl.ds(core, 1), :] - center
    basis = jnp.exp(-2.0 * grid * grid)
    slope = -4.0 * grid * basis
    both = jnp.concatenate([basis.astype(BF16), slope.astype(BF16)], axis=1)
    radial_out = lax.dot_general(
        radial[...], both, (((0,), (0,)), ((), ())), preferred_element_type=F32
    )
    preact = radial_out[:, :128]
    sigma = jax.nn.sigmoid(preact)
    gate[0] = preact * sigma * live
    gate[1] = sigma * (1.0 + preact * (1.0 - sigma)) * live * radial_out[:, 128:]

    eye = (
        lax.broadcasted_iota(jnp.int32, (8, 8), 0) == lax.broadcasted_iota(jnp.int32, (8, 8), 1)
    ).astype(F32)
    for degree in range(7):
        column = jnp.sum(eweight[degree : degree + 1, :] * eye, axis=1, keepdims=True)
        ewcol[degree] = jnp.broadcast_to(column, (8, 128))

    polar, azimuth = ang[0:1, :], ang[1:2, :]
    unit = [jnp.sin(polar) * jnp.cos(azimuth), jnp.sin(polar) * jnp.sin(azimuth), jnp.cos(polar)]

    both_ghosts.wait_recv()
    lent = dot(jnp.concatenate([ghost[0], ghost[1]], axis=1), shot[...])
    for half in range(2):
        at = 128 * half
        s3[half, 0:26] = (base[0:208, at : at + 128] + lent[:, at : at + 128]).reshape(26, 8, 128)
        s3[half, 26:49] = (
            base[208:392, at : at + 128] + lent[0:184, 256 + at : 384 + at]
        ).reshape(23, 8, 128)

    def piece_of(ref, g, first, count):
        start, rows = CHUNKS[g]
        return ref.at[pl.ds(first, count), pl.ds(start, rows)]

    def blocks(g, src, dst, source, first, count, kind, to):
        return remote(
            piece_of(src, g, source, count), piece_of(dst, g, first, count), a_send, a_recv.at[kind, g], (space, to)
        )

    def own_sends(g):
        plans = []
        plans += [(peer(2, 0, c), c, 2) for c in range(2)]
        plans += [(peer(0, 1, c), c, 1) for c in range(2)]
        for c in range(2):
            plans += [(peer(1, 0, c), c, 0), (peer(3, 0, c), c, 0)]
        plans += [(sibling, other, 0)]
        return [blocks(g, snd, every, half, chan, 1, kind, to) for to, half, kind in plans]

    ahead, behind, across = peer(1, 0, core), peer(3, 0, core), peer(0, 1, core)
    paths = [
        (peer(0, 1, 0), 2, 0, ahead),
        (peer(0, 1, 0), 2, 0, behind),
        (peer(2, 0, 0), 2, 0, across),
    ]

    def passed(g, i):
        first, count, kind, to = paths[i]
        return blocks(g, every, every, first, first, count, kind, to)

    def landed(g, kind, count):
        blocks(g, every, every, 0, 0, count, kind, sibling).wait_recv()

    t3[:, 7] = jnp.zeros((2, 8, 128), F32)
    for g in (1, 2, 0):
        for order in ((0,), (1, 2), (3, 4))[g]:
            for degree in range(LEAST[order], 7):
                width = 2 * degree + 1
                at = OFFSET[degree] + order * width
                row = padded_row(row_of(degree, order))
                for half in range(2):
                    t3[half, row] = jnp.sum(
                        r3[half, at : at + width] * s3[half, degree * degree : (degree + 1) ** 2], axis=0
                    )
        first, rows = CHUNKS[g]
        for half in range(2):
            snd[half, first : first + rows] = (
                t3[half, first // 8 : (first + rows) // 8].reshape(rows, 128).astype(BF16)
            )
        every[chan, first : first + rows] = snd[core, first : first + rows]

        for copy in own_sends(g):
            copy.start()

    for g in (1, 2, 0):
        landed(g, 1, 2)
        passed(g, 0).start()
        passed(g, 1).start()
        landed(g, 2, 2)
        passed(g, 2).start()

    both_tables.wait_recv()
    slot_row = lax.broadcasted_iota(jnp.int32, (64, 256), 0)
    atom_lane = lax.broadcasted_iota(jnp.int32, (128, 64), 0)
    for side in range(2):
        slot_hot = (source - (128 + 64 * side) == slot_row).astype(F32).astype(BF16)
        lent_hot = (ghost_g[side, side : side + 1, 0:64] == atom_lane).astype(F32).astype(BF16)
        pushes[:, 128 * side : 128 * side + 128] = dot(lent_hot, slot_hot).T.astype(BF16)
    pushes[:, 256:384] = (nconst[0].astype(F32) - nconst[1].astype(F32)).T.astype(BF16)
    for copy in weights:
        copy.wait_recv()
    for g in (1, 2, 0):
        landed(g, 0, 11)
        first, rows = CHUNKS[g]
        for t in range(first, first + rows, 16):
            pair = every[:, t : t + 16, :].astype(F32).reshape(NC, 2, 8, 128)
            for i in range(2):
                row = t // 8 + i
                if row == 7:
                    continue
                turned = pair[:, i].reshape(128, 128)
                x[row, :, 0:128] = (turned * gate[0]).astype(BF16)
                x[row, :, 128:256] = (turned * gate[1]).astype(BF16)
        if g == 0:
            y = dot(wz[...].reshape(128, 896), x[0:7].reshape(896, 256))
            for c in range(2):
                ob[c, 0:7] = y[64 * c : 64 * c + 56].reshape(7, 8, 256)
        else:
            w, n, lo = ((w1, 6, 8), (w2, 5, 20))[g - 1]
            flat = w[...].reshape(32 * n, 128 * n)
            plus = dot(flat, x[lo : lo + n].reshape(128 * n, 256))
            minus = dot(flat, x[lo + n : lo + 2 * n].reshape(128 * n, 256))
            for c in range(2):
                real, imag = 16 * n * c, 16 * n * c + 8 * n
                ob[c, lo - 1 : lo - 1 + n] = (
                    plus[real : real + 8 * n] - minus[imag : imag + 8 * n]
                ).reshape(n, 8, 256)
                ob[c, lo - 1 + n : lo - 1 + 2 * n] = (
                    minus[real : real + 8 * n] + plus[imag : imag + 8 * n]
                ).reshape(n, 8, 256)
        low, high = ((0, 7), (7, 19), (19, 29))[g]
        rows = pl.ds(low, high - low)
        remote(ob.at[other, rows], orecv.at[rows], o_send, o_recv, (space, sibling)).start()
    swap = remote(ob.at[other], orecv, o_send, o_recv, (space, sibling))

    def turn_back(half, rows):
        for degree in range(7):
            width = 2 * degree + 1
            ahead = back = None
            for order in range(HEIGHT[degree]):
                at = OFFSET[degree] + order * width
                block = r3[half, at : at + width]
                line = rows(row_of(degree, order))
                one, two = block * line[:, :128], block * line[:, 128:]
                ahead = one if ahead is None else ahead + one
                back = two if back is None else back + two
            pf[half, degree * degree : (degree + 1) ** 2] = ahead
            pt[half, degree * degree : (degree + 1) ** 2] = back

    turn_back(core, lambda row: ob[core, row])
    swap.wait_recv()
    turn_back(other, lambda row: orecv[row])

    total = fcoef[...]
    for half in range(2):
        hi, lo = split(pf[half].reshape(392, 128))
        hot = nconst[1, :, 128 * half : 128 * half + 128]
        total = total + dot_nt(
            jnp.concatenate([hi, lo], axis=1), jnp.concatenate([hot, hot], axis=1)
        )
    hidden = total.reshape(49, 8, 128)
    lead = hidden[0]
    sigma = jax.nn.sigmoid(lead)
    energy = ewcol[0] * (lead * sigma)
    grads = [(ewcol[0] * (sigma * (1.0 + lead * (1.0 - sigma))))[None]]
    for degree in range(1, 7):
        block = hidden[degree * degree : (degree + 1) ** 2]
        square = 1.0 + jnp.sum(block * block, axis=0)
        energy = energy + ewcol[degree] * jnp.log(square)
        grads.append((ewcol[degree] * 2.0 / square) * block)
    hi, lo = split(jnp.concatenate(grads, axis=0).reshape(392, 128))
    hot = nconst[1]
    edge_grads = dot(
        jnp.concatenate([hi, lo], axis=1), jnp.concatenate([hot, hot], axis=0)
    )
    parts = []
    for half in range(2):
        block = edge_grads[:, 128 * half : 128 * half + 128].reshape(49, 8, 128)
        parts.append(jnp.sum(jnp.sum(block * pt[half], axis=0), axis=0, keepdims=True))
    parts.append(jnp.sum(energy, axis=0, keepdims=True))
    pull = jnp.concatenate(parts[:2], axis=1)
    push = jnp.concatenate([pull * u for u in unit] + [jnp.zeros((5, 256), F32)], axis=0)
    hi, lo = split(push)
    hilo = jnp.concatenate([hi.astype(F32), lo.astype(F32)], axis=0).astype(BF16)
    part = dot(hilo, pushes[...])
    part = part[0:8] + part[8:16]
    rank = lax.broadcasted_iota(jnp.int32, (8, 128), 0)
    fsend[0] = part[:, 0:128]
    fsend[1] = part[:, 128:256]
    fsend[2] = jnp.where(rank == 3, parts[2], part[:, 256:384])
    halves = remote(fsend, frecv, f_send, f_recv, (space, sibling))
    halves.start()
    both_ghosts.wait_send()
    both_tables.wait_send()
    for copy in weights + [swap]:
        copy.wait_send()
    whole = every.at[pl.ds(0, NC - 1)]
    remote(whole, whole, a_send, a_recv.at[0, 0], (space, sibling)).wait_send()
    halves.wait_recv()
    fsum[...] = fsend[...] + frecv[...]
    red[chip] = fsum[2]

    def deliver(side, slot, where):
        remote(fsum.at[side], red.at[slot], r_send, r_recv, where).start()

    for d in range(8):
        to = lax.rem(chip + 4 + d, 8) * 2 + core
        deliver(0, 8 + chip, (before, to))
        deliver(1, 16 + chip, (after, to))
    for d in (4, 3, 5, 2, 6, 1, 7):
        deliver(2, chip, (space, lax.rem(chip + d, 8) * 2 + core))
    most = red.at[pl.ds(0, 23)]
    all_sums = remote(most, most, r_send, r_recv, (space, sibling))
    all_sums.wait_recv()
    summed = jnp.sum(red[...], axis=0)
    energy_out[...] = summed[3:4]
    force_out[...] = summed[0:3]
    halves.wait_send()
    all_sums.wait_send()


def local(
    features, ghost_index, edge_src, edge_dst, edge_count, rotation, distance, edge_angle,
    radial_weight, conv_zero, conv_one, conv_two, energy_weight,
):
    vmem = pl.BlockSpec(memory_space=pltpu.VMEM)
    arrays = (
        features,
        ghost_index,
        edge_src.reshape(1, 256),
        edge_dst.reshape(1, 256),
        edge_count,
        rotation,
        distance.reshape(2, 128),
        edge_angle,
        radial_weight,
        conv_zero,
        conv_one,
        conv_two,
        energy_weight,
    )
    dma = pltpu.SemaphoreType.DMA
    energy, forces = pl.pallas_call(
        kernel,
        out_shape=(jax.ShapeDtypeStruct((1, 128), F32), jax.ShapeDtypeStruct((3, 128), F32)),
        in_specs=[pl.BlockSpec(memory_space=pl.ANY)] * 13,
        out_specs=(vmem, vmem),
        scratch_shapes=[(pltpu.SMEM if a.shape == (1,) else pltpu.VMEM)(a.shape, a.dtype) for a in arrays]
        + [
            pltpu.VMEM((416, 128), BF16),
            pltpu.VMEM((416, 256), F32),
            pltpu.VMEM((256, 512), BF16),
            pltpu.VMEM((2, 208, 128), BF16),
            pltpu.VMEM((8, 128), jnp.int32),
            pltpu.VMEM((2, 208, 128), BF16),
            pltpu.VMEM((2, 8, 128), jnp.int32),
            pltpu.VMEM((2, 64, 896), BF16),
            pltpu.VMEM((2, 96, 768), BF16),
            pltpu.VMEM((2, 80, 640), BF16),
            pltpu.VMEM((240, 256), F32),
            pltpu.VMEM((2, 235, 8, 128), F32),
            pltpu.VMEM((2, 49, 8, 128), F32),
            pltpu.VMEM((2, 30, 8, 128), F32),
            pltpu.VMEM((2, 240, 128), BF16),
            pltpu.VMEM((NC, 240, 128), BF16),
            pltpu.VMEM((2, 128, 128), F32),
            pltpu.VMEM((30, 128, 256), BF16),
            pltpu.VMEM((2, 29, 8, 256), F32),
            pltpu.VMEM((29, 8, 256), F32),
            pltpu.VMEM((2, 49, 8, 128), F32),
            pltpu.VMEM((2, 49, 8, 128), F32),
            pltpu.VMEM((392, 128), F32),
            pltpu.VMEM((2, 128, 256), BF16),
            pltpu.VMEM((256, 384), BF16),
            pltpu.VMEM((7, 8, 128), F32),
            pltpu.VMEM((24, 8, 128), F32),
            pltpu.VMEM((3, 8, 128), F32),
            pltpu.VMEM((3, 8, 128), F32),
            pltpu.VMEM((3, 8, 128), F32),
            dma((2,)),
            dma((2,)),
            dma((3,)),
            dma((3,)),
            dma,
            dma((3, 3)),
            dma,
            dma,
            dma,
            dma,
            dma,
            dma,
            dma((13,)),
        ],
        compiler_params=pltpu.CompilerParams(
            collective_id=0, has_side_effects=True, vmem_limit_bytes=60 * 1024 * 1024
        ),
        cost_estimate=pl.CostEstimate(flops=400_000_000, bytes_accessed=3_000_000, transcendentals=200_000),
    )(*arrays)
    return (energy.reshape(128), forces)


def solution(mesh):
    in_specs = (
        P(None, "chan", "space"),
        P(None, "space"),
        P("space"),
        P("space"),
        P("space"),
        P(None, "space"),
        P("space"),
        P(None, "space"),
        P(),
        P(None, "chan", None),
        P(None, None, "chan", None),
        P(None, None, "chan", None),
        P(None, "chan"),
    )
    out_specs = (P("space"), P(None, "space"))
    return jax.shard_map(local, mesh=mesh, in_specs=in_specs, out_specs=out_specs, check_vma=False)
```

```python
import jax
import jax.numpy as jnp
from jax import lax
from jax.experimental import pallas as pl
from jax.experimental.pallas import tpu as pltpu
from jax.sharding import PartitionSpec as P

MESH = pl.DeviceIdType.MESH
F32 = jnp.float32
BF16 = jnp.bfloat16
NC = 16
CHUNKS = ((0, 64), (64, 96), (160, 80))
HEIGHT = [min(2 * l + 1, 5) for l in range(7)]
OFFSET = [sum(HEIGHT[m] * (2 * m + 1) for m in range(l)) for l in range(7)]
FIRST = (0, 7, 13, 19, 24)
LEAST = (0, 1, 1, 2, 2)
FETCH_ORDER = (9, 10, 11, 5, 2, 3, 4, 6, 8, 12, 7)


def row_of(degree, order):
    return FIRST[order] + degree - LEAST[order]


def padded_row(row):
    return row if row < 7 else row + 1


def dot(a, b):
    return jnp.dot(a, b, preferred_element_type=F32)


def dot_nt(a, b):
    return lax.dot_general(a, b, (((1,), (1,)), ((), ())), preferred_element_type=F32)


def split(x):
    hi = x.astype(BF16)
    return hi, (x - hi.astype(F32)).astype(BF16)


def kernel(*refs):
    held = refs[:13]
    energy_out, force_out = refs[13:15]
    feat, gidx, esrc, edst, count, rot, dist, ang, radial, wzero, wone, wtwo, eweight = refs[15:28]
    (
        coef, base, shot, mine, mine_g, ghost, ghost_g, wz, w1, w2, rf, r3, s3, t3, snd, every, gate, x, ob, orecv,
        pf, pt, fcoef, nconst, pushes, ewcol, red, fsend, frecv, fsum,
        g_send, g_recv, w_send, w_recv, a_send, a_recv, o_send, o_recv, r_send, r_recv, f_send, f_recv, h_recv,
    ) = refs[28:]
    fetch = [
        pltpu.make_async_copy(src, dst, h_recv.at[i])
        for i, (src, dst) in enumerate(zip(held, refs[15:28]))
    ]
    fetch[0].start()
    fetch[1].start()
    space = lax.axis_index("space")
    chan = lax.axis_index("chan")
    n_space = lax.axis_size("space")
    after = lax.rem(space + 1, n_space)
    before = lax.rem(space + n_space - 1, n_space)
    core = lax.rem(chan, 2)
    other = 1 - core
    sibling = chan + 1 - 2 * core

    def remote(src, dst, send, recv, where):
        return pltpu.make_async_remote_copy(
            src_ref=src, dst_ref=dst, send_sem=send, recv_sem=recv, device_id=where, device_id_type=MESH
        )

    along, deep = lax.div(chan, 4), lax.rem(lax.div(chan, 2), 2)

    def peer(dy, dz, c):
        return lax.rem(along + dy, 4) * 4 + lax.rem(deep + dz, 2) * 2 + c

    chip = lax.div(chan, 2)
    barrier = pltpu.get_barrier_semaphore()

    def greet(where):
        pl.semaphore_signal(barrier, inc=1, device_id=where, device_id_type=MESH)

    greet((after, chan))
    greet((before, chan))
    greet((space, sibling))
    for c in range(2):
        for dy, dz in ((0, 1), (1, 0), (3, 0), (2, 0)):
            greet((space, peer(dy, dz, c)))
    for dy in range(1, 4):
        greet((space, peer(dy, 1, core)))
    for i in FETCH_ORDER:
        fetch[i].start()

    fetch[0].wait()
    fetch[1].wait()
    own = feat[...].astype(F32).reshape(392, 128)
    fcoef[...] = own
    own = jnp.concatenate([own, jnp.zeros((24, 128), F32)], axis=0).astype(BF16)
    coef[...] = own
    lend_row = lax.broadcasted_iota(jnp.int32, (256, 256), 0)
    lend_at = jnp.concatenate(
        [gidx[0:1, :], gidx[0:1, :] + 128, gidx[1:2, :], gidx[1:2, :] + 128], axis=1
    )
    lend_hot = (lend_at == lend_row).astype(F32).astype(BF16)
    lent = dot(jnp.concatenate([own[:208], own[208:]], axis=1), lend_hot).astype(BF16)
    mine[0] = lent[:, :128]
    mine[1] = lent[:, 128:]
    mine_g[...] = jnp.zeros((8, 128), jnp.int32)
    mine_g[0:2, 0:64] = gidx[...]
    pl.semaphore_wait(barrier, 14)

    exchange = [
        remote(mine.at[0], ghost.at[0], g_send.at[0], g_recv.at[0], (after, chan)),
        remote(mine.at[1], ghost.at[1], g_send.at[0], g_recv.at[0], (before, chan)),
        remote(mine_g, ghost_g.at[0], g_send.at[1], g_recv.at[1], (after, chan)),
        remote(mine_g, ghost_g.at[1], g_send.at[1], g_recv.at[1], (before, chan)),
    ]
    both_ghosts = remote(ghost, ghost, g_send.at[0], g_recv.at[0], (after, chan))
    both_tables = remote(ghost_g, ghost_g, g_send.at[1], g_recv.at[1], (after, chan))
    for copy in exchange:
        copy.start()

    for i in (9, 10, 11):
        fetch[i].wait()
    wz[core] = jnp.concatenate(
        [wzero[...].astype(F32).reshape(56, 896), jnp.zeros((8, 896), F32)], axis=0
    ).astype(BF16)
    w1[core] = wone[...].astype(F32).reshape(96, 768).astype(BF16)
    w2[core] = wtwo[...].astype(F32).reshape(80, 640).astype(BF16)
    weights = [
        remote(w.at[core], w.at[core], w_send.at[i], w_recv.at[i], (space, sibling))
        for i, w in enumerate((wz, w1, w2))
    ]
    for copy in weights:
        copy.start()

    fetch[5].wait()
    rf[0:235, :] = rot[...].astype(F32)

    def spread(i, carry):
        for j in range(5):
            row = i * 5 + j
            line = rf[pl.ds(row, 1), :]
            r3[0, row] = jnp.broadcast_to(line[:, :128], (8, 128))
            r3[1, row] = jnp.broadcast_to(line[:, 128:], (8, 128))
        return carry

    lax.fori_loop(0, 47, spread, 0)

    for i in (2, 3, 4, 6, 7, 8, 12):
        fetch[i].wait()
    atom_row = lax.broadcasted_iota(jnp.int32, (128, 256), 0)
    source = esrc[...]
    target_hot = (edst[...] == atom_row).astype(F32)
    source_hot = (source == atom_row).astype(F32)
    nconst[0] = source_hot.astype(BF16)
    nconst[1] = target_hot.astype(BF16)
    base[...] = dot(coef[...], nconst[0])
    slot_row = lax.broadcasted_iota(jnp.int32, (256, 256), 0)
    slot_of = slot_row - 64 * (slot_row // 64) + 64 * (slot_row // 128)
    upper = (slot_row // 64) % 2
    for half in range(2):
        shot[:, 256 * half : 256 * half + 256] = (
            (source - 128 == jnp.where(upper == half, slot_of, -1000)).astype(F32).astype(BF16)
        )

    live = (lax.broadcasted_iota(jnp.int32, (1, 128), 1) + core * 128 < count[0]).astype(F32)
    center = 12.0 * lax.broadcasted_iota(jnp.int32, (512, 128), 0).astype(F32) / 511.0
    grid = dist[pl.ds(core, 1), :] - center
    basis = jnp.exp(-2.0 * grid * grid)
    slope = -4.0 * grid * basis
    both = jnp.concatenate([basis.astype(BF16), slope.astype(BF16)], axis=1)
    radial_out = lax.dot_general(
        radial[...], both, (((0,), (0,)), ((), ())), preferred_element_type=F32
    )
    preact = radial_out[:, :128]
    sigma = jax.nn.sigmoid(preact)
    gate[0] = preact * sigma * live
    gate[1] = sigma * (1.0 + preact * (1.0 - sigma)) * live * radial_out[:, 128:]

    eye = (
        lax.broadcasted_iota(jnp.int32, (8, 8), 0) == lax.broadcasted_iota(jnp.int32, (8, 8), 1)
    ).astype(F32)
    for degree in range(7):
        column = jnp.sum(eweight[degree : degree + 1, :] * eye, axis=1, keepdims=True)
        ewcol[degree] = jnp.broadcast_to(column, (8, 128))

    polar, azimuth = ang[0:1, :], ang[1:2, :]
    unit = [jnp.sin(polar) * jnp.cos(azimuth), jnp.sin(polar) * jnp.sin(azimuth), jnp.cos(polar)]

    both_ghosts.wait_recv()
    lent = dot(jnp.concatenate([ghost[0], ghost[1]], axis=1), shot[...])
    for half in range(2):
        at = 128 * half
        s3[half, 0:26] = (base[0:208, at : at + 128] + lent[:, at : at + 128]).reshape(26, 8, 128)
        s3[half, 26:49] = (
            base[208:392, at : at + 128] + lent[0:184, 256 + at : 384 + at]
        ).reshape(23, 8, 128)

    def piece_of(ref, g, first, count):
        start, rows = CHUNKS[g]
        return ref.at[pl.ds(first, count), pl.ds(start, rows)]

    def blocks(g, src, dst, source, first, count, kind, to):
        return remote(
            piece_of(src, g, source, count), piece_of(dst, g, first, count), a_send, a_recv.at[kind, g], (space, to)
        )

    def own_sends(g):
        plans = []
        plans += [(peer(2, 0, c), c, 2) for c in range(2)]
        plans += [(peer(0, 1, c), c, 1) for c in range(2)]
        for c in range(2):
            plans += [(peer(1, 0, c), c, 0), (peer(3, 0, c), c, 0)]
        plans += [(sibling, other, 0)]
        return [blocks(g, snd, every, half, chan, 1, kind, to) for to, half, kind in plans]

    ahead, behind, across = peer(1, 0, core), peer(3, 0, core), peer(0, 1, core)
    paths = [
        (peer(0, 1, 0), 2, 0, ahead),
        (peer(0, 1, 0), 2, 0, behind),
        (peer(2, 0, 0), 2, 0, across),
    ]

    def passed(g, i):
        first, count, kind, to = paths[i]
        return blocks(g, every, every, first, first, count, kind, to)

    def landed(g, kind, count):
        blocks(g, every, every, 0, 0, count, kind, sibling).wait_recv()

    t3[:, 7] = jnp.zeros((2, 8, 128), F32)
    for g in (2, 1, 0):
        for order in ((0,), (1, 2), (3, 4))[g]:
            for degree in range(LEAST[order], 7):
                width = 2 * degree + 1
                at = OFFSET[degree] + order * width
                row = padded_row(row_of(degree, order))
                for half in range(2):
                    t3[half, row] = jnp.sum(
                        r3[half, at : at + width] * s3[half, degree * degree : (degree + 1) ** 2], axis=0
                    )
        first, rows = CHUNKS[g]
        for half in range(2):
            snd[half, first : first + rows] = (
                t3[half, first // 8 : (first + rows) // 8].reshape(rows, 128).astype(BF16)
            )
        every[chan, first : first + rows] = snd[core, first : first + rows]

        for copy in own_sends(g):
            copy.start()

    for g in (2, 1, 0):
        landed(g, 1, 2)
        passed(g, 0).start()
        passed(g, 1).start()
        landed(g, 2, 2)
        passed(g, 2).start()

    both_tables.wait_recv()
    slot_row = lax.broadcasted_iota(jnp.int32, (64, 256), 0)
    atom_lane = lax.broadcasted_iota(jnp.int32, (128, 64), 0)
    for side in range(2):
        slot_hot = (source - (128 + 64 * side) == slot_row).astype(F32).astype(BF16)
        lent_hot = (ghost_g[side, side : side + 1, 0:64] == atom_lane).astype(F32).astype(BF16)
        pushes[:, 128 * side : 128 * side + 128] = dot(lent_hot, slot_hot).T.astype(BF16)
    pushes[:, 256:384] = (nconst[0].astype(F32) - nconst[1].astype(F32)).T.astype(BF16)
    for copy in weights:
        copy.wait_recv()
    for g in (2, 1, 0):
        landed(g, 0, 11)
        first, rows = CHUNKS[g]
        for t in range(first, first + rows, 16):
            pair = every[:, t : t + 16, :].astype(F32).reshape(NC, 2, 8, 128)
            for i in range(2):
                row = t // 8 + i
                if row == 7:
                    continue
                turned = pair[:, i].reshape(128, 128)
                x[row, :, 0:128] = (turned * gate[0]).astype(BF16)
                x[row, :, 128:256] = (turned * gate[1]).astype(BF16)
        if g == 0:
            y = dot(wz[...].reshape(128, 896), x[0:7].reshape(896, 256))
            for c in range(2):
                ob[c, 0:7] = y[64 * c : 64 * c + 56].reshape(7, 8, 256)
        else:
            w, n, lo = ((w1, 6, 8), (w2, 5, 20))[g - 1]
            flat = w[...].reshape(32 * n, 128 * n)
            plus = dot(flat, x[lo : lo + n].reshape(128 * n, 256))
            minus = dot(flat, x[lo + n : lo + 2 * n].reshape(128 * n, 256))
            for c in range(2):
                real, imag = 16 * n * c, 16 * n * c + 8 * n
                ob[c, lo - 1 : lo - 1 + n] = (
                    plus[real : real + 8 * n] - minus[imag : imag + 8 * n]
                ).reshape(n, 8, 256)
                ob[c, lo - 1 + n : lo - 1 + 2 * n] = (
                    minus[real : real + 8 * n] + plus[imag : imag + 8 * n]
                ).reshape(n, 8, 256)
        low, high = ((0, 7), (7, 19), (19, 29))[g]
        rows = pl.ds(low, high - low)
        remote(ob.at[other, rows], orecv.at[rows], o_send, o_recv, (space, sibling)).start()
    swap = remote(ob.at[other], orecv, o_send, o_recv, (space, sibling))

    def turn_back(half, rows):
        for degree in range(7):
            width = 2 * degree + 1
            ahead = back = None
            for order in range(HEIGHT[degree]):
                at = OFFSET[degree] + order * width
                block = r3[half, at : at + width]
                line = rows(row_of(degree, order))
                one, two = block * line[:, :128], block * line[:, 128:]
                ahead = one if ahead is None else ahead + one
                back = two if back is None else back + two
            pf[half, degree * degree : (degree + 1) ** 2] = ahead
            pt[half, degree * degree : (degree + 1) ** 2] = back

    turn_back(core, lambda row: ob[core, row])
    swap.wait_recv()
    turn_back(other, lambda row: orecv[row])

    total = fcoef[...]
    for half in range(2):
        hi, lo = split(pf[half].reshape(392, 128))
        hot = nconst[1, :, 128 * half : 128 * half + 128]
        total = total + dot_nt(
            jnp.concatenate([hi, lo], axis=1), jnp.concatenate([hot, hot], axis=1)
        )
    hidden = total.reshape(49, 8, 128)
    lead = hidden[0]
    sigma = jax.nn.sigmoid(lead)
    energy = ewcol[0] * (lead * sigma)
    grads = [(ewcol[0] * (sigma * (1.0 + lead * (1.0 - sigma))))[None]]
    for degree in range(1, 7):
        block = hidden[degree * degree : (degree + 1) ** 2]
        square = 1.0 + jnp.sum(block * block, axis=0)
        energy = energy + ewcol[degree] * jnp.log(square)
        grads.append((ewcol[degree] * 2.0 / square) * block)
    hi, lo = split(jnp.concatenate(grads, axis=0).reshape(392, 128))
    hot = nconst[1]
    edge_grads = dot(
        jnp.concatenate([hi, lo], axis=1), jnp.concatenate([hot, hot], axis=0)
    )
    parts = []
    for half in range(2):
        block = edge_grads[:, 128 * half : 128 * half + 128].reshape(49, 8, 128)
        parts.append(jnp.sum(jnp.sum(block * pt[half], axis=0), axis=0, keepdims=True))
    parts.append(jnp.sum(energy, axis=0, keepdims=True))
    pull = jnp.concatenate(parts[:2], axis=1)
    push = jnp.concatenate([pull * u for u in unit] + [jnp.zeros((5, 256), F32)], axis=0)
    hi, lo = split(push)
    hilo = jnp.concatenate([hi.astype(F32), lo.astype(F32)], axis=0).astype(BF16)
    part = dot(hilo, pushes[...])
    part = part[0:8] + part[8:16]
    rank = lax.broadcasted_iota(jnp.int32, (8, 128), 0)
    fsend[0] = part[:, 0:128]
    fsend[1] = part[:, 128:256]
    fsend[2] = jnp.where(rank == 3, parts[2], part[:, 256:384])
    halves = remote(fsend, frecv, f_send, f_recv, (space, sibling))
    halves.start()
    both_ghosts.wait_send()
    both_tables.wait_send()
    for copy in weights + [swap]:
        copy.wait_send()
    whole = every.at[pl.ds(0, NC - 1)]
    remote(whole, whole, a_send, a_recv.at[0, 0], (space, sibling)).wait_send()
    halves.wait_recv()
    fsum[...] = fsend[...] + frecv[...]
    red[chip] = fsum[2]

    def deliver(side, slot, where):
        remote(fsum.at[side], red.at[slot], r_send, r_recv, where).start()

    for d in range(8):
        to = lax.rem(chip + 4 + d, 8) * 2 + core
        deliver(0, 8 + chip, (before, to))
        deliver(1, 16 + chip, (after, to))
    for d in (4, 3, 5, 2, 6, 1, 7):
        deliver(2, chip, (space, lax.rem(chip + d, 8) * 2 + core))
    most = red.at[pl.ds(0, 23)]
    all_sums = remote(most, most, r_send, r_recv, (space, sibling))
    all_sums.wait_recv()
    summed = jnp.sum(red[...], axis=0)
    energy_out[...] = summed[3:4]
    force_out[...] = summed[0:3]
    halves.wait_send()
    all_sums.wait_send()


def local(
    features, ghost_index, edge_src, edge_dst, edge_count, rotation, distance, edge_angle,
    radial_weight, conv_zero, conv_one, conv_two, energy_weight,
):
    vmem = pl.BlockSpec(memory_space=pltpu.VMEM)
    arrays = (
        features,
        ghost_index,
        edge_src.reshape(1, 256),
        edge_dst.reshape(1, 256),
        edge_count,
        rotation,
        distance.reshape(2, 128),
        edge_angle,
        radial_weight,
        conv_zero,
        conv_one,
        conv_two,
        energy_weight,
    )
    dma = pltpu.SemaphoreType.DMA
    energy, forces = pl.pallas_call(
        kernel,
        out_shape=(jax.ShapeDtypeStruct((1, 128), F32), jax.ShapeDtypeStruct((3, 128), F32)),
        in_specs=[pl.BlockSpec(memory_space=pl.ANY)] * 13,
        out_specs=(vmem, vmem),
        scratch_shapes=[(pltpu.SMEM if a.shape == (1,) else pltpu.VMEM)(a.shape, a.dtype) for a in arrays]
        + [
            pltpu.VMEM((416, 128), BF16),
            pltpu.VMEM((416, 256), F32),
            pltpu.VMEM((256, 512), BF16),
            pltpu.VMEM((2, 208, 128), BF16),
            pltpu.VMEM((8, 128), jnp.int32),
            pltpu.VMEM((2, 208, 128), BF16),
            pltpu.VMEM((2, 8, 128), jnp.int32),
            pltpu.VMEM((2, 64, 896), BF16),
            pltpu.VMEM((2, 96, 768), BF16),
            pltpu.VMEM((2, 80, 640), BF16),
            pltpu.VMEM((240, 256), F32),
            pltpu.VMEM((2, 235, 8, 128), F32),
            pltpu.VMEM((2, 49, 8, 128), F32),
            pltpu.VMEM((2, 30, 8, 128), F32),
            pltpu.VMEM((2, 240, 128), BF16),
            pltpu.VMEM((NC, 240, 128), BF16),
            pltpu.VMEM((2, 128, 128), F32),
            pltpu.VMEM((30, 128, 256), BF16),
            pltpu.VMEM((2, 29, 8, 256), F32),
            pltpu.VMEM((29, 8, 256), F32),
            pltpu.VMEM((2, 49, 8, 128), F32),
            pltpu.VMEM((2, 49, 8, 128), F32),
            pltpu.VMEM((392, 128), F32),
            pltpu.VMEM((2, 128, 256), BF16),
            pltpu.VMEM((256, 384), BF16),
            pltpu.VMEM((7, 8, 128), F32),
            pltpu.VMEM((24, 8, 128), F32),
            pltpu.VMEM((3, 8, 128), F32),
            pltpu.VMEM((3, 8, 128), F32),
            pltpu.VMEM((3, 8, 128), F32),
            dma((2,)),
            dma((2,)),
            dma((3,)),
            dma((3,)),
            dma,
            dma((3, 3)),
            dma,
            dma,
            dma,
            dma,
            dma,
            dma,
            dma((13,)),
        ],
        compiler_params=pltpu.CompilerParams(
            collective_id=0, has_side_effects=True, vmem_limit_bytes=60 * 1024 * 1024
        ),
        cost_estimate=pl.CostEstimate(flops=400_000_000, bytes_accessed=3_000_000, transcendentals=200_000),
    )(*arrays)
    return (energy.reshape(128), forces)


def solution(mesh):
    in_specs = (
        P(None, "chan", "space"),
        P(None, "space"),
        P("space"),
        P("space"),
        P("space"),
        P(None, "space"),
        P("space"),
        P(None, "space"),
        P(),
        P(None, "chan", None),
        P(None, None, "chan", None),
        P(None, None, "chan", None),
        P(None, "chan"),
    )
    out_specs = (P("space"), P(None, "space"))
    return jax.shard_map(local, mesh=mesh, in_specs=in_specs, out_specs=out_specs, check_vma=False)
```

```python
import jax
import jax.numpy as jnp
from jax import lax
from jax.experimental import pallas as pl
from jax.experimental.pallas import tpu as pltpu
from jax.sharding import PartitionSpec as P

MESH = pl.DeviceIdType.MESH
F32 = jnp.float32
BF16 = jnp.bfloat16
NC = 16
CHUNKS = ((0, 64), (64, 96), (160, 80))
HEIGHT = [min(2 * l + 1, 5) for l in range(7)]
OFFSET = [sum(HEIGHT[m] * (2 * m + 1) for m in range(l)) for l in range(7)]
FIRST = (0, 7, 13, 19, 24)
LEAST = (0, 1, 1, 2, 2)
FETCH_ORDER = (9, 10, 11, 5, 2, 3, 4, 6, 8, 12, 7)


def row_of(degree, order):
    return FIRST[order] + degree - LEAST[order]


def padded_row(row):
    return row if row < 7 else row + 1


def dot(a, b):
    return jnp.dot(a, b, preferred_element_type=F32)


def dot_nt(a, b):
    return lax.dot_general(a, b, (((1,), (1,)), ((), ())), preferred_element_type=F32)


def split(x):
    hi = x.astype(BF16)
    return hi, (x - hi.astype(F32)).astype(BF16)


def kernel(*refs):
    held = refs[:13]
    energy_out, force_out = refs[13:15]
    feat, gidx, esrc, edst, count, rot, dist, ang, radial, wzero, wone, wtwo, eweight = refs[15:28]
    (
        coef, base, shot, mine, mine_g, ghost, ghost_g, wz, w1, w2, rf, r3, s3, t3, snd, every, gate, x, ob, orecv,
        pf, pt, fcoef, nconst, pushes, ewcol, red, fsend, frecv, fsum,
        g_send, g_recv, w_send, w_recv, a_send, a_recv, o_send, o_recv, r_send, r_recv, f_send, f_recv, h_recv,
    ) = refs[28:]
    fetch = [
        pltpu.make_async_copy(src, dst, h_recv.at[i])
        for i, (src, dst) in enumerate(zip(held, refs[15:28]))
    ]
    fetch[0].start()
    fetch[1].start()
    space = lax.axis_index("space")
    chan = lax.axis_index("chan")
    n_space = lax.axis_size("space")
    after = lax.rem(space + 1, n_space)
    before = lax.rem(space + n_space - 1, n_space)
    core = lax.rem(chan, 2)
    other = 1 - core
    sibling = chan + 1 - 2 * core

    def remote(src, dst, send, recv, where):
        return pltpu.make_async_remote_copy(
            src_ref=src, dst_ref=dst, send_sem=send, recv_sem=recv, device_id=where, device_id_type=MESH
        )

    along, deep = lax.div(chan, 4), lax.rem(lax.div(chan, 2), 2)

    def peer(dy, dz, c):
        return lax.rem(along + dy, 4) * 4 + lax.rem(deep + dz, 2) * 2 + c

    chip = lax.div(chan, 2)
    barrier = pltpu.get_barrier_semaphore()

    def greet(where):
        pl.semaphore_signal(barrier, inc=1, device_id=where, device_id_type=MESH)

    greet((after, chan))
    greet((before, chan))
    greet((space, sibling))
    for c in range(2):
        for dy, dz in ((0, 1), (1, 0), (3, 0), (2, 0)):
            greet((space, peer(dy, dz, c)))
    for dy in range(1, 4):
        greet((space, peer(dy, 1, core)))
    for i in FETCH_ORDER:
        fetch[i].start()

    fetch[0].wait()
    fetch[1].wait()
    own = feat[...].astype(F32).reshape(392, 128)
    fcoef[...] = own
    own = jnp.concatenate([own, jnp.zeros((24, 128), F32)], axis=0).astype(BF16)
    coef[...] = own
    lend_row = lax.broadcasted_iota(jnp.int32, (256, 256), 0)
    lend_at = jnp.concatenate(
        [gidx[0:1, :], gidx[0:1, :] + 128, gidx[1:2, :], gidx[1:2, :] + 128], axis=1
    )
    lend_hot = (lend_at == lend_row).astype(F32).astype(BF16)
    lent = dot(jnp.concatenate([own[:208], own[208:]], axis=1), lend_hot).astype(BF16)
    mine[0] = lent[:, :128]
    mine[1] = lent[:, 128:]
    mine_g[...] = jnp.zeros((8, 128), jnp.int32)
    mine_g[0:2, 0:64] = gidx[...]
    pl.semaphore_wait(barrier, 14)

    exchange = [
        remote(mine.at[0], ghost.at[0], g_send.at[0], g_recv.at[0], (after, chan)),
        remote(mine.at[1], ghost.at[1], g_send.at[0], g_recv.at[0], (before, chan)),
        remote(mine_g, ghost_g.at[0], g_send.at[1], g_recv.at[1], (after, chan)),
        remote(mine_g, ghost_g.at[1], g_send.at[1], g_recv.at[1], (before, chan)),
    ]
    both_ghosts = remote(ghost, ghost, g_send.at[0], g_recv.at[0], (after, chan))
    both_tables = remote(ghost_g, ghost_g, g_send.at[1], g_recv.at[1], (after, chan))
    for copy in exchange:
        copy.start()

    for i in (9, 10, 11):
        fetch[i].wait()
    wz[core] = jnp.concatenate(
        [wzero[...].astype(F32).reshape(56, 896), jnp.zeros((8, 896), F32)], axis=0
    ).astype(BF16)
    w1[core] = wone[...].astype(F32).reshape(96, 768).astype(BF16)
    w2[core] = wtwo[...].astype(F32).reshape(80, 640).astype(BF16)
    weights = [
        remote(w.at[core], w.at[core], w_send.at[i], w_recv.at[i], (space, sibling))
        for i, w in enumerate((wz, w1, w2))
    ]
    for copy in weights:
        copy.start()

    fetch[5].wait()
    rf[0:235, :] = rot[...].astype(F32)

    def spread(i, carry):
        for j in range(5):
            row = i * 5 + j
            line = rf[pl.ds(row, 1), :]
            r3[0, row] = jnp.broadcast_to(line[:, :128], (8, 128))
            r3[1, row] = jnp.broadcast_to(line[:, 128:], (8, 128))
        return carry

    lax.fori_loop(0, 47, spread, 0)

    for i in (2, 3, 4, 6, 7, 8, 12):
        fetch[i].wait()
    atom_row = lax.broadcasted_iota(jnp.int32, (128, 256), 0)
    source = esrc[...]
    target_hot = (edst[...] == atom_row).astype(F32)
    source_hot = (source == atom_row).astype(F32)
    nconst[0] = source_hot.astype(BF16)
    nconst[1] = target_hot.astype(BF16)
    base[...] = dot(coef[...], nconst[0])
    slot_row = lax.broadcasted_iota(jnp.int32, (256, 256), 0)
    slot_of = slot_row - 64 * (slot_row // 64) + 64 * (slot_row // 128)
    upper = (slot_row // 64) % 2
    for half in range(2):
        shot[:, 256 * half : 256 * half + 256] = (
            (source - 128 == jnp.where(upper == half, slot_of, -1000)).astype(F32).astype(BF16)
        )

    live = (lax.broadcasted_iota(jnp.int32, (1, 128), 1) + core * 128 < count[0]).astype(F32)
    center = 12.0 * lax.broadcasted_iota(jnp.int32, (512, 128), 0).astype(F32) / 511.0
    grid = dist[pl.ds(core, 1), :] - center
    basis = jnp.exp(-2.0 * grid * grid)
    slope = -4.0 * grid * basis
    both = jnp.concatenate([basis.astype(BF16), slope.astype(BF16)], axis=1)
    radial_out = lax.dot_general(
        radial[...], both, (((0,), (0,)), ((), ())), preferred_element_type=F32
    )
    preact = radial_out[:, :128]
    sigma = jax.nn.sigmoid(preact)
    gate[0] = preact * sigma * live
    gate[1] = sigma * (1.0 + preact * (1.0 - sigma)) * live * radial_out[:, 128:]

    eye = (
        lax.broadcasted_iota(jnp.int32, (8, 8), 0) == lax.broadcasted_iota(jnp.int32, (8, 8), 1)
    ).astype(F32)
    for degree in range(7):
        column = jnp.sum(eweight[degree : degree + 1, :] * eye, axis=1, keepdims=True)
        ewcol[degree] = jnp.broadcast_to(column, (8, 128))

    polar, azimuth = ang[0:1, :], ang[1:2, :]
    unit = [jnp.sin(polar) * jnp.cos(azimuth), jnp.sin(polar) * jnp.sin(azimuth), jnp.cos(polar)]

    both_ghosts.wait_recv()
    lent = dot(jnp.concatenate([ghost[0], ghost[1]], axis=1), shot[...])
    for half in range(2):
        at = 128 * half
        s3[half, 0:26] = (base[0:208, at : at + 128] + lent[:, at : at + 128]).reshape(26, 8, 128)
        s3[half, 26:49] = (
            base[208:392, at : at + 128] + lent[0:184, 256 + at : 384 + at]
        ).reshape(23, 8, 128)

    def piece_of(ref, g, first, count):
        start, rows = CHUNKS[g]
        return ref.at[pl.ds(first, count), pl.ds(start, rows)]

    def blocks(g, src, dst, source, first, count, kind, to):
        return remote(
            piece_of(src, g, source, count), piece_of(dst, g, first, count), a_send, a_recv.at[kind, g], (space, to)
        )

    def own_sends(g):
        plans = []
        plans += [(peer(2, 0, c), c, 2) for c in range(2)]
        plans += [(peer(0, 1, c), c, 1) for c in range(2)]
        for c in range(2):
            plans += [(peer(1, 0, c), c, 0), (peer(3, 0, c), c, 0)]
        plans += [(sibling, other, 0)]
        return [blocks(g, snd, every, half, chan, 1, kind, to) for to, half, kind in plans]

    ahead, behind, across = peer(1, 0, core), peer(3, 0, core), peer(0, 1, core)
    paths = [
        (peer(0, 1, 0), 2, 0, ahead),
        (peer(0, 1, 0), 2, 0, behind),
        (peer(2, 0, 0), 2, 0, across),
    ]

    def passed(g, i):
        first, count, kind, to = paths[i]
        return blocks(g, every, every, first, first, count, kind, to)

    def landed(g, kind, count):
        blocks(g, every, every, 0, 0, count, kind, sibling).wait_recv()

    t3[:, 7] = jnp.zeros((2, 8, 128), F32)
    for g in (2, 1, 0):
        for order in ((0,), (1, 2), (3, 4))[g]:
            for degree in range(LEAST[order], 7):
                width = 2 * degree + 1
                at = OFFSET[degree] + order * width
                row = padded_row(row_of(degree, order))
                for half in range(2):
                    t3[half, row] = jnp.sum(
                        r3[half, at : at + width] * s3[half, degree * degree : (degree + 1) ** 2], axis=0
                    )
        first, rows = CHUNKS[g]
        for half in range(2):
            snd[half, first : first + rows] = (
                t3[half, first // 8 : (first + rows) // 8].reshape(rows, 128).astype(BF16)
            )
        every[chan, first : first + rows] = snd[core, first : first + rows]

        for copy in own_sends(g)[:4]:
            copy.start()

    for g in (2, 1, 0):
        for copy in own_sends(g)[4:]:
            copy.start()
    for g in (2, 1, 0):
        landed(g, 1, 2)
        passed(g, 0).start()
        passed(g, 1).start()
        landed(g, 2, 2)
        passed(g, 2).start()

    both_tables.wait_recv()
    slot_row = lax.broadcasted_iota(jnp.int32, (64, 256), 0)
    atom_lane = lax.broadcasted_iota(jnp.int32, (128, 64), 0)
    for side in range(2):
        slot_hot = (source - (128 + 64 * side) == slot_row).astype(F32).astype(BF16)
        lent_hot = (ghost_g[side, side : side + 1, 0:64] == atom_lane).astype(F32).astype(BF16)
        pushes[:, 128 * side : 128 * side + 128] = dot(lent_hot, slot_hot).T.astype(BF16)
    pushes[:, 256:384] = (nconst[0].astype(F32) - nconst[1].astype(F32)).T.astype(BF16)
    for copy in weights:
        copy.wait_recv()
    for g in (2, 1, 0):
        landed(g, 0, 11)
        first, rows = CHUNKS[g]
        for t in range(first, first + rows, 16):
            pair = every[:, t : t + 16, :].astype(F32).reshape(NC, 2, 8, 128)
            for i in range(2):
                row = t // 8 + i
                if row == 7:
                    continue
                turned = pair[:, i].reshape(128, 128)
                x[row, :, 0:128] = (turned * gate[0]).astype(BF16)
                x[row, :, 128:256] = (turned * gate[1]).astype(BF16)
        if g == 0:
            y = dot(wz[...].reshape(128, 896), x[0:7].reshape(896, 256))
            for c in range(2):
                ob[c, 0:7] = y[64 * c : 64 * c + 56].reshape(7, 8, 256)
        else:
            w, n, lo = ((w1, 6, 8), (w2, 5, 20))[g - 1]
            flat = w[...].reshape(32 * n, 128 * n)
            plus = dot(flat, x[lo : lo + n].reshape(128 * n, 256))
            minus = dot(flat, x[lo + n : lo + 2 * n].reshape(128 * n, 256))
            for c in range(2):
                real, imag = 16 * n * c, 16 * n * c + 8 * n
                ob[c, lo - 1 : lo - 1 + n] = (
                    plus[real : real + 8 * n] - minus[imag : imag + 8 * n]
                ).reshape(n, 8, 256)
                ob[c, lo - 1 + n : lo - 1 + 2 * n] = (
                    minus[real : real + 8 * n] + plus[imag : imag + 8 * n]
                ).reshape(n, 8, 256)
        low, high = ((0, 7), (7, 19), (19, 29))[g]
        rows = pl.ds(low, high - low)
        remote(ob.at[other, rows], orecv.at[rows], o_send, o_recv, (space, sibling)).start()
    swap = remote(ob.at[other], orecv, o_send, o_recv, (space, sibling))

    def turn_back(half, rows):
        for degree in range(7):
            width = 2 * degree + 1
            ahead = back = None
            for order in range(HEIGHT[degree]):
                at = OFFSET[degree] + order * width
                block = r3[half, at : at + width]
                line = rows(row_of(degree, order))
                one, two = block * line[:, :128], block * line[:, 128:]
                ahead = one if ahead is None else ahead + one
                back = two if back is None else back + two
            pf[half, degree * degree : (degree + 1) ** 2] = ahead
            pt[half, degree * degree : (degree + 1) ** 2] = back

    turn_back(core, lambda row: ob[core, row])
    swap.wait_recv()
    turn_back(other, lambda row: orecv[row])

    total = fcoef[...]
    for half in range(2):
        hi, lo = split(pf[half].reshape(392, 128))
        hot = nconst[1, :, 128 * half : 128 * half + 128]
        total = total + dot_nt(
            jnp.concatenate([hi, lo], axis=1), jnp.concatenate([hot, hot], axis=1)
        )
    hidden = total.reshape(49, 8, 128)
    lead = hidden[0]
    sigma = jax.nn.sigmoid(lead)
    energy = ewcol[0] * (lead * sigma)
    grads = [(ewcol[0] * (sigma * (1.0 + lead * (1.0 - sigma))))[None]]
    for degree in range(1, 7):
        block = hidden[degree * degree : (degree + 1) ** 2]
        square = 1.0 + jnp.sum(block * block, axis=0)
        energy = energy + ewcol[degree] * jnp.log(square)
        grads.append((ewcol[degree] * 2.0 / square) * block)
    hi, lo = split(jnp.concatenate(grads, axis=0).reshape(392, 128))
    hot = nconst[1]
    edge_grads = dot(
        jnp.concatenate([hi, lo], axis=1), jnp.concatenate([hot, hot], axis=0)
    )
    parts = []
    for half in range(2):
        block = edge_grads[:, 128 * half : 128 * half + 128].reshape(49, 8, 128)
        parts.append(jnp.sum(jnp.sum(block * pt[half], axis=0), axis=0, keepdims=True))
    parts.append(jnp.sum(energy, axis=0, keepdims=True))
    pull = jnp.concatenate(parts[:2], axis=1)
    push = jnp.concatenate([pull * u for u in unit] + [jnp.zeros((5, 256), F32)], axis=0)
    hi, lo = split(push)
    hilo = jnp.concatenate([hi.astype(F32), lo.astype(F32)], axis=0).astype(BF16)
    part = dot(hilo, pushes[...])
    part = part[0:8] + part[8:16]
    rank = lax.broadcasted_iota(jnp.int32, (8, 128), 0)
    fsend[0] = part[:, 0:128]
    fsend[1] = part[:, 128:256]
    fsend[2] = jnp.where(rank == 3, parts[2], part[:, 256:384])
    halves = remote(fsend, frecv, f_send, f_recv, (space, sibling))
    halves.start()
    both_ghosts.wait_send()
    both_tables.wait_send()
    for copy in weights + [swap]:
        copy.wait_send()
    whole = every.at[pl.ds(0, NC - 1)]
    remote(whole, whole, a_send, a_recv.at[0, 0], (space, sibling)).wait_send()
    halves.wait_recv()
    fsum[...] = fsend[...] + frecv[...]
    red[chip] = fsum[2]

    def deliver(side, slot, where):
        remote(fsum.at[side], red.at[slot], r_send, r_recv, where).start()

    for d in range(8):
        to = lax.rem(chip + 4 + d, 8) * 2 + core
        deliver(0, 8 + chip, (before, to))
        deliver(1, 16 + chip, (after, to))
    for d in (4, 3, 5, 2, 6, 1, 7):
        deliver(2, chip, (space, lax.rem(chip + d, 8) * 2 + core))
    most = red.at[pl.ds(0, 23)]
    all_sums = remote(most, most, r_send, r_recv, (space, sibling))
    all_sums.wait_recv()
    summed = jnp.sum(red[...], axis=0)
    energy_out[...] = summed[3:4]
    force_out[...] = summed[0:3]
    halves.wait_send()
    all_sums.wait_send()


def local(
    features, ghost_index, edge_src, edge_dst, edge_count, rotation, distance, edge_angle,
    radial_weight, conv_zero, conv_one, conv_two, energy_weight,
):
    vmem = pl.BlockSpec(memory_space=pltpu.VMEM)
    arrays = (
        features,
        ghost_index,
        edge_src.reshape(1, 256),
        edge_dst.reshape(1, 256),
        edge_count,
        rotation,
        distance.reshape(2, 128),
        edge_angle,
        radial_weight,
        conv_zero,
        conv_one,
        conv_two,
        energy_weight,
    )
    dma = pltpu.SemaphoreType.DMA
    energy, forces = pl.pallas_call(
        kernel,
        out_shape=(jax.ShapeDtypeStruct((1, 128), F32), jax.ShapeDtypeStruct((3, 128), F32)),
        in_specs=[pl.BlockSpec(memory_space=pl.ANY)] * 13,
        out_specs=(vmem, vmem),
        scratch_shapes=[(pltpu.SMEM if a.shape == (1,) else pltpu.VMEM)(a.shape, a.dtype) for a in arrays]
        + [
            pltpu.VMEM((416, 128), BF16),
            pltpu.VMEM((416, 256), F32),
            pltpu.VMEM((256, 512), BF16),
            pltpu.VMEM((2, 208, 128), BF16),
            pltpu.VMEM((8, 128), jnp.int32),
            pltpu.VMEM((2, 208, 128), BF16),
            pltpu.VMEM((2, 8, 128), jnp.int32),
            pltpu.VMEM((2, 64, 896), BF16),
            pltpu.VMEM((2, 96, 768), BF16),
            pltpu.VMEM((2, 80, 640), BF16),
            pltpu.VMEM((240, 256), F32),
            pltpu.VMEM((2, 235, 8, 128), F32),
            pltpu.VMEM((2, 49, 8, 128), F32),
            pltpu.VMEM((2, 30, 8, 128), F32),
            pltpu.VMEM((2, 240, 128), BF16),
            pltpu.VMEM((NC, 240, 128), BF16),
            pltpu.VMEM((2, 128, 128), F32),
            pltpu.VMEM((30, 128, 256), BF16),
            pltpu.VMEM((2, 29, 8, 256), F32),
            pltpu.VMEM((29, 8, 256), F32),
            pltpu.VMEM((2, 49, 8, 128), F32),
            pltpu.VMEM((2, 49, 8, 128), F32),
            pltpu.VMEM((392, 128), F32),
            pltpu.VMEM((2, 128, 256), BF16),
            pltpu.VMEM((256, 384), BF16),
            pltpu.VMEM((7, 8, 128), F32),
            pltpu.VMEM((24, 8, 128), F32),
            pltpu.VMEM((3, 8, 128), F32),
            pltpu.VMEM((3, 8, 128), F32),
            pltpu.VMEM((3, 8, 128), F32),
            dma((2,)),
            dma((2,)),
            dma((3,)),
            dma((3,)),
            dma,
            dma((3, 3)),
            dma,
            dma,
            dma,
            dma,
            dma,
            dma,
            dma((13,)),
        ],
        compiler_params=pltpu.CompilerParams(
            collective_id=0, has_side_effects=True, vmem_limit_bytes=60 * 1024 * 1024
        ),
        cost_estimate=pl.CostEstimate(flops=400_000_000, bytes_accessed=3_000_000, transcendentals=200_000),
    )(*arrays)
    return (energy.reshape(128), forces)


def solution(mesh):
    in_specs = (
        P(None, "chan", "space"),
        P(None, "space"),
        P("space"),
        P("space"),
        P("space"),
        P(None, "space"),
        P("space"),
        P(None, "space"),
        P(),
        P(None, "chan", None),
        P(None, None, "chan", None),
        P(None, None, "chan", None),
        P(None, "chan"),
    )
    out_specs = (P("space"), P(None, "space"))
    return jax.shard_map(local, mesh=mesh, in_specs=in_specs, out_specs=out_specs, check_vma=False)
```
